512 devices in a mesh: dp: 8 (over y, core), expert: 64 (over x, z).
Axes of the slice: x: 4, y: 4, z: 16, core: 2. Of those that a mesh axis runs over, the one named last changes fastest.
Arguments:
- tokens: bfloat16 [65536, 2048], P(('dp', 'expert')), may hold values from -6 to 6
- gate_values: float32 [65536, 6], P(('dp', 'expert')), may hold values from 0.03 to 0.5
- expert_ids: int32 [65536, 6], P(('dp', 'expert')), may hold values from 0 to 63, all different within a row; in each aligned block of 128 rows (0 to 127, 128 to 255, ...) at most 16 rows name the same one
- down_weight: bfloat16 [2048, 512], P('expert'), may hold values from -0.125 to 0.125
- up_weight: bfloat16 [2048, 512], P('expert'), may hold values from -0.125 to 0.125
- expert_gate: bfloat16 [64, 512, 768], P('expert'), may hold values from -0.25 to 0.25
- expert_up: bfloat16 [64, 512, 768], P('expert'), may hold values from -0.25 to 0.25
- expert_down: bfloat16 [64, 768, 512], P('expert'), may hold values from -0.21875 to 0.21875
- out_grad: bfloat16 [65536, 2048], P(('dp', 'expert')), may hold values from -24 to 24
Outputs:
- input_grad: bfloat16 [65536, 2048], P(('dp', 'expert'))
- up_grad: float32 [2048, 512], P('expert')
The draws below stay inside these ranges and needn't reach their ends.
Inputs may be any that keep to these rules, and one draw needn't show every extreme that they name: `expert_ids`: the 6 experts of a token differ. Among the rows of one device (aligned blocks of 128 tokens) no expert is named more than 16 times, a bound that some block reaches.
All inputs are finite; a program needn't handle non-finite values.
Results may differ from the reference program's by a relative error of at most 0.011.
Values may be sent and summed in bfloat16 or wider, within the bound.
A program may use at most 64 MiB of HBM per device.

```python
import math
import jax
import jax.numpy as jnp
import numpy as np
from jax import lax

D = 2048
LATENT = 512
HIDDEN_SIZE = 768
TOP = 6
TOK_DEV = 128
EXPERTS = 64
CAP = 16
TOKENS = 65536
N_DP = 8
N_EXPERT = 64


def raised(values, own_key, source, target, parts, factor):
    owner, partner = [(jnp.arange(values.shape[axis_at]) // (values.shape[axis_at] // parts)).reshape([-1 if axis == axis_at else 1 for axis in range(values.ndim)]) for axis_at in (source, target)]
    chosen = jax.random.permutation(own_key, parts)[partner]
    strong = (owner == chosen) | (owner == (partner + parts // 2) % parts)
    return jnp.where(strong, factor * values, values)


def block_scale(own_key, extent, cuts, least, high):
    def one(axis_at, blocks):
        draws = jax.random.uniform(jax.random.fold_in(jax.random.fold_in(own_key, 6), axis_at), (blocks,), jnp.float32, least / len(cuts), high / len(cuts))
        return jnp.repeat(jnp.exp(draws), extent[axis_at] // blocks).reshape((-1,) + (1,) * (len(extent) - axis_at - 1))

    loudness = one(*cuts[0])
    for cut in cuts[1:]:
        loudness = loudness * one(*cut)
    return loudness


def routed_block(own_key, own, number, rows, number_of, top, limit, slope):
    ranking = jax.random.permutation(own_key, number_of)
    crowded, common = shares(number_of, rows * top, limit, slope, True), shares(number_of, rows * top, limit, slope, False)
    places = jnp.arange(number_of)

    def named(sizes, offset_by):
        used = int((sizes > 0).sum())
        fixed = max(1, used // 4)
        passed = fixed + (places - fixed + offset_by * (used - fixed)) % max(1, number_of - fixed)
        return jnp.zeros((number_of,), jnp.int32).at[ranking[jnp.where(places < fixed, places, passed)]].set(jnp.asarray(sizes, jnp.int32))

    sizes = jnp.where(number % 4 == 0, named(crowded, number // 4), named(common, number - number // 4 - 1))
    mixed = jax.random.permutation(jax.random.fold_in(own, 3), number_of)
    source_of, taker = mixed[0:number_of // 2 * 2:2], mixed[1:number_of // 2 * 2:2]
    slack = jnp.minimum(sizes[source_of] - 1, limit - sizes[taker]) // 2
    slack = jnp.where((source_of == ranking[0]) | (taker == ranking[0]) | (sizes[taker] == 0), 0, jnp.maximum(slack, 0))
    passed = jax.random.randint(jax.random.fold_in(own, 4), (number_of // 2,), 0, 1 << 20) % (slack + 1)
    sizes = sizes.at[source_of].add(-passed).at[taker].add(passed)
    items = jnp.searchsorted(jnp.cumsum(sizes), jnp.arange(rows * top), side="right").astype(jnp.int32)
    table = items.reshape(top, rows).T
    table = table[jax.random.permutation(jax.random.fold_in(own, 1), rows)]
    offset_by = jax.random.randint(jax.random.fold_in(own, 2), (rows, 1), 0, top)
    return jnp.take_along_axis(table, (jnp.arange(top)[None, :] + offset_by) % top, axis=1)


def shares(number_of, total, bound, skew, full):
    portions = [(1 << 20) // math.isqrt(grade ** skew) + 1 for grade in range(1, number_of + 1)]
    largest = bound if full else min(bound, max(-(-total // number_of), total * portions[0] // sum(portions)))
    least = 1 if total - largest >= number_of - 1 else 0
    given, surplus = [largest] + [least] * (number_of - 1), total - largest - least * (number_of - 1)
    while surplus > 0:
        candidates = [i for i in range(1, number_of) if given[i] < largest] or [i for i in range(1, number_of) if given[i] < bound]
        mass, left = sum([portions[i] for i in candidates]), surplus
        for i in candidates:
            extra = min(bound - given[i], max(1, left * portions[i] // mass), surplus)
            given[i] = given[i] + extra
            surplus = surplus - extra
    return np.array(given)


def scatter_about(key, dims, width, limit, pieces=(), held_as=jnp.bfloat16):
    array = width * jax.random.normal(key, dims, jnp.float32)
    if pieces:
        array = array * block_scale(key, dims, pieces, -0.22, 0.18)
    return jnp.clip(array, -limit, limit).astype(held_as)


def gaussian_with(own_key, extent, deviation, bound, split, heavy, kind=jnp.bfloat16):
    array = deviation * jax.random.normal(own_key, extent, jnp.float32)
    if split:
        array = array * block_scale(own_key, extent, split, -0.22, 0.18)
    return jnp.clip(raised(array, jax.random.fold_in(own_key, 3), *heavy), -bound, bound).astype(kind)


def setup_inputs(seed: int = 0) -> dict:
    splits = jax.random.split(jax.random.key(seed), 10)
    tokens = scatter_about(splits[0], (TOKENS, D), 1.0, 6.0, ((0, 512),))
    gate_values = jnp.clip(jnp.exp(math.log(0.5) - 2.8134107 * jax.random.uniform(splits[1], (TOKENS, TOP), jnp.float32) ** block_scale(splits[1], (TOKENS, TOP), ((0, 512),), -0.2, 0.2)), 0.03, 0.5)
    expert_ids_keys = jax.random.split(jax.random.fold_in(splits[2], 1), TOKENS // TOK_DEV)
    expert_ids_turns = jax.random.permutation(jax.random.fold_in(splits[2], 3), TOKENS // TOK_DEV)
    expert_ids = jax.vmap(lambda own, number: routed_block(jax.random.fold_in(splits[2], 2), own, number, TOK_DEV, EXPERTS, TOP, CAP, 2))(expert_ids_keys, expert_ids_turns).reshape((TOKENS, TOP))
    down_weight = scatter_about(splits[3], (D, LATENT), D ** -0.5, 0.125, ((0, 64),))
    up_weight = scatter_about(splits[4], (D, LATENT), D ** -0.5, 0.125, ((0, 64),))
    expert_gate = scatter_about(splits[5], (EXPERTS, LATENT, HIDDEN_SIZE), LATENT ** -0.5, 0.25, ((0, 64),))
    expert_up = scatter_about(splits[6], (EXPERTS, LATENT, HIDDEN_SIZE), LATENT ** -0.5, 0.25, ((0, 64),))
    expert_down = scatter_about(splits[7], (EXPERTS, HIDDEN_SIZE, LATENT), HIDDEN_SIZE ** -0.5, 0.21875, ((0, 64),))
    out_grad = gaussian_with(splits[8], (TOKENS, D), 1.0, 24.0, ((0, 512),), (0, 1, 512, 6.0))
    return dict(tokens=tokens, gate_values=gate_values, expert_ids=expert_ids, down_weight=down_weight, up_weight=up_weight, expert_gate=expert_gate, expert_up=expert_up, expert_down=expert_down, out_grad=out_grad)


def expert_pre(rows, gate_w, up_w):
    gate_pre = jnp.dot(rows, gate_w, preferred_element_type=jnp.float32)
    up_pre = jnp.dot(rows, up_w, preferred_element_type=jnp.float32)
    return (gate_pre, up_pre)

def reference(tokens, gate_values, expert_ids, down_weight, up_weight, expert_gate, expert_up, expert_down, out_grad):
    latent = jnp.dot(tokens, down_weight, preferred_element_type=jnp.float32).astype(jnp.bfloat16)
    flat_ids = expert_ids.reshape(-1).astype(jnp.int32)
    flat_gates = gate_values.reshape(-1)
    order = jnp.argsort(flat_ids, stable=True).astype(jnp.int32)
    counts = jax.ops.segment_sum(jnp.ones_like(flat_ids), flat_ids, num_segments=EXPERTS).astype(jnp.int32)
    starts = (jnp.cumsum(counts) - counts).astype(jnp.int32)
    most = N_DP * N_EXPERT * CAP
    padded = jnp.concatenate([order, jnp.zeros((most,), jnp.int32)])
    expert_list = jnp.arange(EXPERTS, dtype=jnp.int32)

    def select(index):
        picks = lax.dynamic_slice(padded, (starts[index],), (most,)).astype(jnp.int32)
        valid = jnp.arange(most, dtype=jnp.int32) < counts[index]
        owners = (picks // TOP).astype(jnp.int32)
        rows = jnp.where(valid[:, None], latent[owners], jnp.zeros((), jnp.bfloat16))
        return (picks, valid, owners, rows)

    def forward_step(total, index):
        picks, valid, owners, rows = select(index)
        gate_pre, up_pre = expert_pre(rows, expert_gate[index], expert_up[index])
        hidden = (jax.nn.silu(gate_pre) * up_pre).astype(jnp.bfloat16)
        result = jnp.dot(hidden, expert_down[index], preferred_element_type=jnp.float32).astype(jnp.bfloat16)
        weight = jnp.where(valid, flat_gates[picks], jnp.zeros((), jnp.float32))
        return (total.at[owners].add(result.astype(jnp.float32) * weight[:, None]), None)
    combined, unused = lax.scan(forward_step, jnp.zeros((TOKENS, LATENT), jnp.float32), expert_list)
    combined = combined.astype(jnp.bfloat16)
    latent_cot = jnp.dot(out_grad, up_weight, preferred_element_type=jnp.float32)
    up_grad = lax.dot_general(out_grad, combined, (((0,), (0,)), ((), ())), preferred_element_type=jnp.float32)
    up_grad = up_grad * (1.0 / math.sqrt(TOKENS))

    def backward_step(total, index):
        picks, valid, owners, rows = select(index)
        gate_pre, up_pre = expert_pre(rows, expert_gate[index], expert_up[index])
        weight = jnp.where(valid, flat_gates[picks], jnp.zeros((), jnp.float32))
        slot_cot = (weight[:, None] * latent_cot[owners]).astype(jnp.bfloat16)
        hidden_cot = lax.dot_general(slot_cot, expert_down[index], (((1,), (1,)), ((), ())), preferred_element_type=jnp.float32)
        sig = jax.nn.sigmoid(gate_pre)
        gate_cot = (hidden_cot * up_pre * sig * (1.0 + gate_pre * (1.0 - sig))).astype(jnp.bfloat16)
        up_cot = (hidden_cot * gate_pre * sig).astype(jnp.bfloat16)
        back = lax.dot_general(gate_cot, expert_gate[index], (((1,), (1,)), ((), ())), preferred_element_type=jnp.float32)
        back = back + lax.dot_general(up_cot, expert_up[index], (((1,), (1,)), ((), ())), preferred_element_type=jnp.float32)
        back = back.astype(jnp.bfloat16).astype(jnp.float32)
        back = jnp.where(valid[:, None], back, jnp.zeros((), jnp.float32))
        return (total.at[owners].add(back), None)
    latent_grad, unused = lax.scan(backward_step, jnp.zeros((TOKENS, LATENT), jnp.float32), expert_list)
    latent_grad = latent_grad.astype(jnp.bfloat16)
    input_grad = lax.dot_general(latent_grad, down_weight, (((1,), (1,)), ((), ())), preferred_element_type=jnp.float32)
    return (input_grad.astype(jnp.bfloat16), up_grad)
```

```python
import functools
import math

import jax
import jax.numpy as jnp
from jax import lax
from jax.experimental import pallas as pl
from jax.experimental.pallas import tpu as pltpu
from jax.sharding import PartitionSpec as P

CORES = 2
F32 = jnp.float32
BF16 = jnp.bfloat16


class Place:
    def __init__(self, sizes):
        self.xs, self.ys, self.zs = sizes
        dp, ex = lax.axis_index("dp"), lax.axis_index("expert")
        self.y, self.c = dp // CORES, dp % CORES
        self.x, self.z = ex // self.zs, ex % self.zs

    def at(self, x=None, y=None, z=None, c=None):
        x = self.x if x is None else x
        y = self.y if y is None else y
        z = self.z if z is None else z
        c = self.c if c is None else c
        return (y * CORES + c, x * self.zs + z)


def send(src, dst, send_sem, recv_sem, device):
    pltpu.make_async_remote_copy(
        src_ref=src,
        dst_ref=dst,
        send_sem=send_sem,
        recv_sem=recv_sem,
        device_id=device,
        device_id_type=pl.DeviceIdType.MESH,
    ).start()


def wait(ref, sem):
    pltpu.make_async_copy(ref, ref, sem).wait()


def rows(start, size):
    return pl.ds(pl.multiple_of(start, size), size)


def project_kernel(
    sizes, tokens, out_grad, down, up, lc, wd,
    shard, w4, both, res,
    local_sem, pair_send, pair_recv, z_send, z_recv, x_send, x_recv, y_send, y_recv, f_recv, d_send, d_recv,
):
    me = Place(sizes)
    x, y, z, c = me.x, me.y, me.z, me.c
    other = 1 - c
    shard_rows, tok = down.shape[0], tokens.shape[0]
    block = shard_rows * me.zs
    peer = me.at(c=other)

    mine = both.at[rows(c * tok, tok)]

    @pl.when(c == 0)
    def _():
        send(out_grad, mine, pair_send.at[0], pair_recv.at[0], peer)
        pltpu.make_async_copy(tokens, mine, local_sem.at[0]).start()
        shard[...] = down[...]

    @pl.when(c == 1)
    def _():
        send(tokens, mine, pair_send.at[0], pair_recv.at[0], peer)
        pltpu.make_async_copy(out_grad, mine, local_sem.at[0]).start()
        shard[...] = up[...]

    part = w4.at[y, rows((x * me.zs + z) * shard_rows, shard_rows)]
    part[...] = shard[:, pl.ds(pl.multiple_of(y * 128, 128), 128)]
    for dz in range(1, me.zs):
        send(part, part, z_send, z_recv, me.at(z=(z + dz) % me.zs))
    others = w4.at[0, pl.ds(0, block - shard_rows)]
    wait(others, z_recv)

    own = w4.at[y, rows(x * block, block)]
    for dx in range(1, me.xs):
        send(own, own, x_send, x_recv.at[dx], me.at(x=(x + dx) % me.xs))
    hops = (1, me.ys - 1)
    for dx in range(me.xs):
        held = w4.at[y, rows((x + me.xs - dx) % me.xs * block, block)]
        if dx:
            wait(held, x_recv.at[dx])
        for way, dy in enumerate(hops):
            send(held, held, y_send, y_recv.at[way, dx], me.at(y=(y + dy) % me.ys))
    for dx in range(me.xs):
        for way, dy in enumerate(hops):
            source = (y + me.ys - dy) % me.ys
            got = w4.at[source, rows((x + me.xs - dx) % me.xs * block, block)]
            wait(got, y_recv.at[way, dx])
            if dx // (me.xs // 2) == way:
                send(got, got, y_send, f_recv.at[dx], me.at(y=(y + dy) % me.ys))

    wait(mine, local_sem.at[0])
    wait(mine, pair_recv.at[0])

    def project(col):
        value = jnp.dot(both[...], w4[col], preferred_element_type=F32).astype(BF16)
        res[col] = value

    for dy in (0, 1, me.ys - 1):
        project((y + dy) % me.ys)
    far = (y + me.ys // 2) % me.ys
    for dx in range(me.xs):
        wait(w4.at[far, rows((x + me.xs - dx) % me.xs * block, block)], f_recv.at[dx])
    project(far)
    for col in range(me.ys):
        lc[c, :, pl.ds(col * 128, 128)] = res[col, rows(c * tok, tok), :]
    for col in range(me.ys):
        send(
            res.at[col, rows(other * tok, tok)], lc.at[c, :, pl.ds(col * 128, 128)],
            pair_send.at[1], pair_recv.at[1], peer,
        )

    @pl.when(c == 0)
    def _():
        send(w4, wd, d_send, d_recv, peer)
        pltpu.make_async_copy(w4, wd, local_sem.at[1]).start()
        wait(wd, local_sem.at[1])
        wait(wd, d_send)

    wait(lc.at[c], pair_recv.at[1])
    wait(lc.at[c], pair_send.at[1])

    @pl.when(c == 1)
    def _():
        wait(wd, d_recv)

    wait(mine, pair_send.at[0])
    wait(others, z_send)
    for _ in range(1, me.xs):
        wait(own, x_send)
    for _ in range(2 * me.xs + me.xs):
        wait(own, y_send)


def project(sizes, tokens, out_grad, down, up):
    xs, ys, zs = sizes
    tok, width = tokens.shape
    latent = down.shape[1]
    vmem = pl.BlockSpec(memory_space=pltpu.VMEM)
    hbm = pl.BlockSpec(memory_space=pl.ANY)
    dma = pltpu.SemaphoreType.DMA
    return pl.pallas_call(
        functools.partial(project_kernel, sizes),
        out_shape=(
            jax.ShapeDtypeStruct((2, tok, latent), BF16),
            jax.ShapeDtypeStruct((ys, width, 128), BF16),
        ),
        in_specs=[hbm, hbm, vmem, vmem],
        out_specs=(vmem, vmem),
        scratch_shapes=[
            pltpu.VMEM(down.shape, BF16),
            pltpu.VMEM((ys, width, 128), BF16),
            pltpu.VMEM((2 * tok, width), BF16),
            pltpu.VMEM((ys, 2 * tok, 128), BF16),
            dma((2,)), dma((2,)), dma((2,)), dma(()), dma(()), dma(()), dma((xs,)),
            dma(()), dma((2, xs)), dma((xs,)), dma(()), dma(()),
        ],
        compiler_params=pltpu.CompilerParams(has_side_effects=True, vmem_limit_bytes=48 * 2**20),
        name="project",
    )(tokens, out_grad, down, up)


def up_grad_kernel(
    sizes, scale, out_grad, combined, out,
    og, cb, term, rx, s1, ry, s2, rz,
    pair_send, pair_recv, local_sem, x_send, x_recv, y_send, y_recv, z_send, z_recv, o_send, o_recv,
):
    me = Place(sizes)
    x, y, z, c = me.x, me.y, me.z, me.c
    xs, ys, zs = sizes
    tok = combined.shape[0]
    shard_rows = out.shape[0]
    block = shard_rows * zs
    half = out.shape[1] // CORES
    peer = me.at(c=1 - c)
    mine = rows(c * tok, tok)

    send(out_grad, og.at[mine], pair_send.at[0], pair_recv.at[0], peer)
    send(combined, cb.at[mine], pair_send.at[1], pair_recv.at[1], peer)
    pltpu.make_async_copy(out_grad, og.at[mine], local_sem).start()
    cb[mine, :] = combined[...]
    wait(og.at[mine], local_sem)
    wait(og.at[mine], pair_recv.at[0])
    wait(cb.at[mine], pair_recv.at[1])
    columns = cb[:, pl.ds(pl.multiple_of(c * half, 128), half)]

    own = None
    for dx in (1, xs - 1) + tuple(range(2, xs - 1)) + (0,):
        to = (x + dx) % xs
        value = lax.dot_general(
            og[:, pl.ds(pl.multiple_of(to * block, 128), block)], columns,
            (((0,), (0,)), ((), ())), preferred_element_type=F32,
        )
        if dx:
            term[dx] = value.astype(BF16)
            send(term.at[dx], rx.at[dx], x_send, x_recv.at[dx], me.at(x=to))
        else:
            own = value
    total = own
    for dx in range(1, xs):
        wait(rx.at[dx], x_recv.at[dx])
        total = total + rx[dx].astype(F32)
    s1[...] = total.reshape(zs // ys, ys, shard_rows, half).astype(BF16)

    for dy in range(1, ys):
        to = (y + dy) % ys
        for q in range(zs // ys):
            send(s1.at[q, to], ry.at[dy, q], y_send, y_recv.at[dy], me.at(y=to))
    total = s1[:, y].astype(F32)
    for dy in range(1, ys):
        wait(ry.at[dy], y_recv.at[dy])
        total = total + ry[dy].astype(F32)
    s2[...] = total.astype(BF16)

    owner = z % ys == y
    for q in range(zs // ys):
        to = q * ys + y

        @pl.when(to != z)
        def _():
            send(s2.at[q], rz.at[z], z_send, z_recv, me.at(z=to))

        @pl.when(to == z)
        def _():
            rz[z] = s2[q]

    cols = pl.ds(pl.multiple_of(c * half, 128), half)

    @pl.when(owner)
    def _():
        wait(rz.at[pl.ds(0, zs - 1)], z_recv)
        total = rz[0].astype(F32)
        for source in range(1, zs):
            total = total + rz[source].astype(F32)
        out[:, cols] = total * scale
        for dy in range(ys):
            for dc in range(CORES):
                if dy or dc:
                    send(
                        out.at[:, cols], out.at[:, cols], o_send, o_recv.at[c],
                        me.at(y=(y + dy) % ys, c=(c + dc) % CORES),
                    )
        for _ in range(ys * CORES - 1):
            wait(out.at[:, cols], o_send)
        wait(s2.at[pl.ds(0, zs // ys - 1)], z_send)
        there = pl.ds(pl.multiple_of((1 - c) * half, 128), half)
        wait(out.at[:, there], o_recv.at[1 - c])

    @pl.when(jnp.logical_not(owner))
    def _():
        for core in range(CORES):
            wait(out.at[:, pl.ds(core * half, half)], o_recv.at[core])
        wait(s2, z_send)

    wait(og.at[mine], pair_send.at[0])
    wait(cb.at[mine], pair_send.at[1])
    wait(rx.at[pl.ds(1, xs - 1)], x_send)
    wait(ry.at[pl.ds(1, ys - 1)], y_send)


def up_gradient(sizes, out_grad, combined, shard_rows, total_tokens):
    xs, ys, zs = sizes
    tok, width = out_grad.shape
    latent = combined.shape[1]
    half = latent // CORES
    block = shard_rows * zs
    vmem = pl.BlockSpec(memory_space=pltpu.VMEM)
    hbm = pl.BlockSpec(memory_space=pl.ANY)
    dma = pltpu.SemaphoreType.DMA
    return pl.pallas_call(
        functools.partial(up_grad_kernel, sizes, 1.0 / math.sqrt(total_tokens)),
        out_shape=jax.ShapeDtypeStruct((shard_rows, latent), F32),
        in_specs=[hbm, vmem],
        out_specs=vmem,
        scratch_shapes=[
            pltpu.VMEM((2 * tok, width), BF16),
            pltpu.VMEM((2 * tok, latent), BF16),
            pltpu.VMEM((xs, block, half), BF16),
            pltpu.VMEM((xs, block, half), BF16),
            pltpu.VMEM((zs // ys, ys, shard_rows, half), BF16),
            pltpu.VMEM((ys, zs // ys, shard_rows, half), BF16),
            pltpu.VMEM((zs // ys, shard_rows, half), BF16),
            pltpu.VMEM((zs, shard_rows, half), BF16),
            dma((2,)), dma((2,)), dma(()), dma(()), dma((xs,)), dma(()), dma((ys,)),
            dma(()), dma(()), dma(()), dma((CORES,)),
        ],
        compiler_params=pltpu.CompilerParams(has_side_effects=True, vmem_limit_bytes=48 * 2**20),
        name="up_gradient",
    )(out_grad, combined)


def slot_targets(expert_ids, experts, capacity):
    flat_ids = expert_ids.reshape(-1)
    onehot = (flat_ids[:, None] == jnp.arange(experts, dtype=jnp.int32)[None, :]).astype(jnp.int32)
    before = jnp.cumsum(onehot, axis=0) - onehot
    places = jnp.sum(before * onehot, axis=1)
    return flat_ids * capacity + places


def route(payload, targets, experts, capacity, work):
    width = payload.shape[1]
    buffer = jnp.zeros((experts * capacity, width), payload.dtype).at[targets].set(payload)
    arrived = lax.all_to_all(
        buffer.reshape(experts, capacity, width), "expert", split_axis=0, concat_axis=0, tiled=True
    )
    result, saved = work(arrived.reshape(experts * capacity, width))
    returned = lax.all_to_all(
        result.reshape(experts, capacity, width), "expert", split_axis=0, concat_axis=0, tiled=True
    )
    return (returned.reshape(experts * capacity, width)[targets], saved)


def contract_last(left, right):
    return lax.dot_general(
        left, right, (((1,), (1,)), ((), ())), preferred_element_type=jnp.float32
    )


def local(
    sizes,
    tokens,
    gate_values,
    expert_ids,
    down_weight,
    up_weight,
    expert_gate,
    expert_up,
    expert_down,
    out_grad,
):
    experts = lax.axis_size("expert")
    tok_count, top_count = expert_ids.shape
    capacity = max(2, 4 * tok_count * top_count // (3 * experts))
    width = down_weight.shape[1]
    owned_rows = down_weight.shape[0]
    total_tokens = tok_count * lax.axis_size("dp") * experts
    targets = slot_targets(expert_ids, experts, capacity)
    lc, wd = project(sizes, tokens, out_grad, down_weight, up_weight)
    latent = lc[0]
    latent_cot = lc[1].astype(F32)
    w_gate = expert_gate[0]
    w_up = expert_up[0]
    w_down = expert_down[0]

    def forward_work(rows):
        gate_pre = jnp.dot(rows, w_gate, preferred_element_type=jnp.float32)
        up_pre = jnp.dot(rows, w_up, preferred_element_type=jnp.float32)
        hidden = (jax.nn.silu(gate_pre) * up_pre).astype(jnp.bfloat16)
        result = jnp.dot(hidden, w_down, preferred_element_type=jnp.float32).astype(jnp.bfloat16)
        return (result, (gate_pre, up_pre))

    def backward_work(rows, saved):
        gate_pre, up_pre = saved
        hidden_cot = contract_last(rows, w_down)
        sig = jax.nn.sigmoid(gate_pre)
        gate_cot = (hidden_cot * up_pre * sig * (1.0 + gate_pre * (1.0 - sig))).astype(jnp.bfloat16)
        up_cot = (hidden_cot * gate_pre * sig).astype(jnp.bfloat16)
        back = contract_last(gate_cot, w_gate) + contract_last(up_cot, w_up)
        return back.astype(jnp.bfloat16)

    repeated = jnp.broadcast_to(latent[:, None, :], (tok_count, top_count, width)).reshape(
        tok_count * top_count, width
    )
    slot_cot = (
        (gate_values[:, :, None] * latent_cot[:, None, :])
        .reshape(tok_count * top_count, width)
        .astype(jnp.bfloat16)
    )
    picked, saved = route(repeated, targets, experts, capacity, forward_work)

    def backward_route(rows):
        return (backward_work(rows, saved), None)

    picked_cot, unused = route(slot_cot, targets, experts, capacity, backward_route)
    weighted = (
        picked.astype(jnp.float32).reshape(tok_count, top_count, width) * gate_values[:, :, None]
    )
    combined = jnp.sum(weighted, axis=1).astype(jnp.bfloat16)
    up_grad = up_gradient(sizes, out_grad, combined, owned_rows, total_tokens)
    latent_grad = jnp.sum(
        picked_cot.astype(jnp.float32).reshape(tok_count, top_count, width), axis=1
    ).astype(jnp.bfloat16)
    input_grad = lax.dot_general(
        latent_grad.reshape(tok_count, -1, 128), wd, (((1, 2), (0, 2)), ((), ())),
        preferred_element_type=jnp.float32,
    )
    return (input_grad.astype(jnp.bfloat16), up_grad)


def solution(mesh):
    dp, ex = mesh.shape["dp"], mesh.shape["expert"]
    ys = dp // CORES
    sizes = (ys, ys, ex // ys)
    return jax.shard_map(
        functools.partial(local, sizes),
        mesh=mesh,
        in_specs=(
            P(("dp", "expert"), None),
            P(("dp", "expert"), None),
            P(("dp", "expert"), None),
            P("expert", None),
            P("expert", None),
            P("expert", None, None),
            P("expert", None, None),
            P("expert", None, None),
            P(("dp", "expert"), None),
        ),
        out_specs=(P(("dp", "expert"), None), P("expert", None)),
        check_vma=False,
    )
```

```python
import functools
import math

import jax
import jax.numpy as jnp
from jax import lax
from jax.experimental import pallas as pl
from jax.experimental.pallas import tpu as pltpu
from jax.sharding import PartitionSpec as P

CORES = 2
SLAB = 2
LANES = 128
CHUNKS = 8
AHEAD = 4
F32 = jnp.float32
BF16 = jnp.bfloat16


class Place:
    def __init__(self, sizes):
        self.xs, self.ys, self.zs = sizes
        dp, ex = lax.axis_index("dp"), lax.axis_index("expert")
        self.y, self.c = dp // CORES, dp % CORES
        self.x, self.z = ex // self.zs, ex % self.zs
        self.half = self.z % SLAB
        self.index = (self.x * self.ys + self.y) * CORES + self.c
        self.plane = self.xs * self.ys * CORES

    def at(self, x=None, y=None, z=None, c=None):
        x = self.x if x is None else x
        y = self.y if y is None else y
        z = self.z if z is None else z
        c = self.c if c is None else c
        return (y * CORES + c, x * self.zs + z)

    def in_plane(self, index):
        c, y, x = index % CORES, index // CORES % self.ys, index // (CORES * self.ys)
        return self.at(x=x, y=y, c=c)


def send(src, dst, send_sem, recv_sem, device):
    pltpu.make_async_remote_copy(
        src_ref=src,
        dst_ref=dst,
        send_sem=send_sem,
        recv_sem=recv_sem,
        device_id=device,
        device_id_type=pl.DeviceIdType.MESH,
    ).start()


def wait(ref, sem):
    pltpu.make_async_copy(ref, ref, sem).wait()


def rows(start, size):
    return pl.ds(pl.multiple_of(start, size), size)


def dot(left, right, left_axis=1, right_axis=0):
    return lax.dot_general(
        left, right, (((left_axis,), (right_axis,)), ((), ())), preferred_element_type=F32
    )


class Weights:
    def __init__(self, me, pairs, send_sem, recv_sem):
        self.me, self.pairs, self.send_sem, self.recv_sem = me, pairs, send_sem, recv_sem
        zs = me.zs
        spread = zs // (CORES * SLAB)
        base = me.z + zs - me.y - spread * me.c
        self.owns = base % (zs // SLAB) == 0
        which = base % zs // (zs // SLAB)
        self.same = jnp.logical_and(self.owns, which == me.half)
        self.first = jnp.where(which == me.half, 2, 1)
        away = (base + zs - (zs // SLAB) * me.half) % zs
        self.up = jnp.logical_and(away > 0, away + 2 <= zs // 2)
        self.down = away > zs // 2 + 2
        self.done = 0
        for i in range(AHEAD):
            self.begin(i)

    def piece(self, i):
        src, dst = self.pairs[i // CHUNKS]
        size = dst.shape[0] // CHUNKS
        part = pl.ds(i % CHUNKS * size, size)
        return src.at[0, part], dst.at[part]

    def begin(self, i):
        me = self.me
        if i >= CHUNKS * len(self.pairs):
            return
        src, dst = self.piece(i)

        @pl.when(self.owns)
        def _():
            send(src, dst, self.send_sem, self.recv_sem.at[i], me.at(z=(me.z + self.first) % me.zs))
            send(src, dst, self.send_sem, self.recv_sem.at[i], me.at(z=(me.z + me.zs - self.first) % me.zs))

        @pl.when(self.same)
        def _():
            pltpu.make_async_copy(src, dst, self.recv_sem.at[i]).start()

    def step(self, count=1):
        me = self.me
        for _ in range(count):
            i = self.done
            if i >= CHUNKS * len(self.pairs):
                return
            self.done += 1
            self.begin(i + AHEAD)
            dst = self.piece(i)[1]
            wait(dst, self.recv_sem.at[i])

            @pl.when(self.up)
            def _():
                send(dst, dst, self.send_sem, self.recv_sem.at[i], me.at(z=(me.z + 2) % me.zs))

            @pl.when(self.down)
            def _():
                send(dst, dst, self.send_sem, self.recv_sem.at[i], me.at(z=(me.z + me.zs - 2) % me.zs))

    def finish(self):
        def sent():
            for _, dst in self.pairs:
                wait(dst, self.send_sem)

        @pl.when(self.owns)
        def _():
            sent()
            sent()

        @pl.when(jnp.logical_or(self.up, self.down))
        def _():
            sent()


def layer_kernel(
    sizes, cap, scale,
    tokens, out_grad, gates, ids, down, up, w_gate, w_up, w_down,
    in_grad, up_grad,
    shard, w4, wd, both, og, res, lc, gate2, ids2, pick, high, low, outbox, inbox, wg, wu, wn,
    gate_pre, up_pre, result, back, ret, ret2, part, got, cb, term, rx, s1, ry, s2, rz,
    local_sem, pair_send, pair_recv, z_send, z_recv, x_send, x_recv, y_send, y_recv, f_recv, w_send, w_recv,
    n_send, n_recv, s_send, s_recv, r_send, r_recv, p_send, p_recv,
    gx_send, gx_recv, gy_send, gy_recv, gz_send, gz_recv, go_send, go_recv,
):
    me = Place(sizes)
    xs, ys, zs = sizes
    x, y, z, c, half = me.x, me.y, me.z, me.c, me.half
    other = 1 - c
    shard_rows, latent = down.shape
    tok, width = tokens.shape
    block = shard_rows * zs
    peer = me.at(c=other)
    partner = me.at(z=z + 1 - 2 * half)
    plane = me.plane
    top = ids.shape[1]
    mine = rows(c * tok, tok)

    @pl.when(c == 0)
    def _():
        send(out_grad, both.at[mine], pair_send.at[0], pair_recv.at[0], peer)
        pltpu.make_async_copy(tokens, both.at[mine], local_sem.at[0]).start()
        shard[...] = down[...]

    @pl.when(c == 1)
    def _():
        send(tokens, both.at[mine], pair_send.at[0], pair_recv.at[0], peer)
        pltpu.make_async_copy(out_grad, both.at[mine], local_sem.at[0]).start()
        shard[...] = up[...]

    piece = w4.at[y, rows((x * zs + z) * shard_rows, shard_rows)]
    piece[...] = shard[:, pl.ds(pl.multiple_of(y * LANES, LANES), LANES)]
    for dz in range(1, zs):
        send(piece, piece, z_send, z_recv, me.at(z=(z + dz) % zs))
    send(gates, gate2.at[half], n_send.at[0], n_recv.at[0], partner)
    send(ids, ids2.at[half], n_send.at[1], n_recv.at[1], partner)
    weights = Weights(me, ((w_gate, wg), (w_up, wu), (w_down, wn)), w_send, w_recv)
    send(out_grad, og.at[mine], pair_send.at[2], pair_recv.at[2], peer)
    pltpu.make_async_copy(out_grad, og.at[mine], local_sem.at[2]).start()
    gate2[half] = gates[...]
    ids2[half] = ids[...]
    others = w4.at[0, pl.ds(0, block - shard_rows)]
    wait(others, z_recv)

    own = w4.at[y, rows(x * block, block)]
    for dx in range(1, xs):
        send(own, own, x_send, x_recv.at[dx], me.at(x=(x + dx) % xs))
    hops = (1, ys - 1)
    for dx in range(xs):
        held = w4.at[y, rows((x + xs - dx) % xs * block, block)]
        if dx:
            wait(held, x_recv.at[dx])
        for way, dy in enumerate(hops):
            send(held, held, y_send, y_recv.at[way, dx], me.at(y=(y + dy) % ys))
        weights.step()

    wait(gates, n_recv.at[0])
    wait(ids, n_recv.at[1])
    slots = plane * cap
    lane = lax.broadcasted_iota(jnp.int32, (1, slots), 1)
    seat, index = lane % cap, lane // cap
    spread = zs // (CORES * SLAB)
    expert = (
        index // (CORES * ys) * zs + index // CORES % ys + spread * (index % CORES) + (zs // SLAB) * half
    )
    before = (
        lax.broadcasted_iota(jnp.int32, (tok, tok), 1) < lax.broadcasted_iota(jnp.int32, (tok, tok), 0)
    ).astype(BF16)
    for q in range(SLAB):
        named = jnp.zeros((tok, slots), F32)
        gate = jnp.zeros((tok, slots), F32)
        for k in range(top):
            hit = ids2[q, :, k : k + 1] == expert
            named = jnp.where(hit, 1.0, named)
            gate = jnp.where(hit, gate2[q, :, k : k + 1], gate)
        place = dot(before, named.astype(BF16))
        chosen = jnp.where(place == seat.astype(F32), named, 0.0)
        gate = gate * chosen
        head = gate.astype(BF16)
        pick[q] = chosen.astype(BF16)
        high[q] = head
        low[q] = (gate - head.astype(F32)).astype(BF16)

    for dx in range(xs):
        for way, dy in enumerate(hops):
            source = (y + ys - dy) % ys
            block_in = w4.at[source, rows((x + xs - dx) % xs * block, block)]
            wait(block_in, y_recv.at[way, dx])
            if dx // (xs // 2) == way:
                send(block_in, block_in, y_send, f_recv.at[dx], me.at(y=(y + dy) % ys))
        weights.step()

    wait(both.at[mine], local_sem.at[0])
    wait(both.at[mine], pair_recv.at[0])

    def project(col):
        value = dot(both[...], w4[col]).astype(BF16)
        res[col] = value

    for dy in (0, 1, ys - 1):
        project((y + dy) % ys)
    far = (y + ys // 2) % ys
    for dx in range(xs):
        wait(w4.at[far, rows((x + xs - dx) % xs * block, block)], f_recv.at[dx])
    project(far)

    def lanes(col):
        return pl.ds(pl.multiple_of(c * latent + col * LANES, LANES), LANES)

    for col in range(ys):
        send(res.at[col, rows(other * tok, tok)], lc.at[half, :, lanes(col)], pair_send.at[1], pair_recv.at[1], peer)
    for col in range(ys):
        lc[half, :, lanes(col)] = res[col, mine, :]

    @pl.when(c == 0)
    def _():
        send(w4, wd, pair_send.at[3], pair_recv.at[3], peer)
        pltpu.make_async_copy(w4, wd, local_sem.at[1]).start()

    quarter = lc.at[half, :, pl.ds(0, latent)]
    wait(quarter, pair_recv.at[1])
    send(lc.at[half], lc.at[half], n_send.at[2], n_recv.at[2], partner)

    def dispatch(q):
        tile = 8
        def fill(t, _):
            part_lanes = pl.ds(pl.multiple_of(t * tile * cap, tile * cap), tile * cap)
            picked = dot(pick[q, :, part_lanes], lc[q, :, :latent], 0, 0)
            cot = dot(high[q, :, part_lanes], lc[q, :, latent:], 0, 0) + dot(
                low[q, :, part_lanes], lc[q, :, latent:], 0, 0
            )
            outbox[q, pl.ds(t * tile, tile), :, :latent] = picked.astype(BF16).reshape(tile, cap, latent)
            outbox[q, pl.ds(t * tile, tile), :, latent:] = cot.astype(BF16).reshape(tile, cap, latent)
            return 0
        lax.fori_loop(0, plane // tile, fill, 0)
        def post(d, _):
            to = (me.index + d) % plane
            send(outbox.at[q, to], inbox.at[me.index, q], s_send, s_recv, me.in_plane(to))
            return 0
        lax.fori_loop(1, plane, post, 0)
        inbox[me.index, q] = outbox[q, me.index]

    dispatch(half)
    weights.step(2)
    wait(lc.at[0], n_recv.at[2])
    dispatch(1 - half)
    weights.step(CHUNKS * 3)
    wait(inbox.at[pl.ds(0, plane - 1)], s_recv)

    group = 8
    size = group * SLAB * cap

    def tile_of(t):
        return (t + me.index // group) % (plane // group)

    def post_back(box, ret_box, which, g):
        def post(d, _):
            to = g * group + d
            @pl.when(to != me.index)
            def _():
                send(box.at[to], ret_box.at[me.index], r_send.at[which], r_recv.at[which], me.in_plane(to))
            @pl.when(to == me.index)
            def _():
                ret_box[to] = box[to]
            return 0
        lax.fori_loop(0, group, post, 0)

    def forward(t, _):
        g = tile_of(t)
        box, span = pl.ds(g * group, group), rows(g * size, size)
        value = inbox[box, :, :, :latent].reshape(size, latent)
        pre = dot(value, wg[...])
        pre_up = dot(value, wu[...])
        gate_pre[span, :] = pre
        up_pre[span, :] = pre_up
        hidden = (pre * jax.nn.sigmoid(pre) * pre_up).astype(BF16)
        result[box] = dot(hidden, wn[...]).astype(BF16).reshape(group, SLAB, cap, latent)
        post_back(result, ret, 0, g)
        return 0

    lax.fori_loop(0, plane // group, forward, 0)

    def backward(t, _):
        g = tile_of(t)
        box, span = pl.ds(g * group, group), rows(g * size, size)
        value = inbox[box, :, :, latent:].reshape(size, latent)
        hidden_cot = dot(value, wn[...], 1, 1)
        pre, pre_up = gate_pre[span, :], up_pre[span, :]
        sig = jax.nn.sigmoid(pre)
        gate_cot = (hidden_cot * pre_up * sig * (1.0 + pre * (1.0 - sig))).astype(BF16)
        up_cot = (hidden_cot * pre * sig).astype(BF16)
        total = dot(gate_cot, wg[...], 1, 1) + dot(up_cot, wu[...], 1, 1)
        back[box] = total.astype(BF16).reshape(group, SLAB, cap, latent)
        post_back(back, ret2, 1, g)
        return 0

    lax.fori_loop(0, plane // group, backward, 0)

    def gather_back(which, box, weigh):
        wait(box.at[pl.ds(0, plane - 1)], r_recv.at[which])
        def total(q):
            value = box[:, q].reshape(slots, latent)
            return sum(dot(m[q], value) for m in weigh)
        part[which] = total(1 - half).astype(BF16)
        send(part.at[which], got.at[which], p_send.at[which], p_recv.at[which], partner)
        own_part = total(half)
        wait(got.at[which], p_recv.at[which])
        return (own_part + got[which].astype(F32)).astype(BF16)

    cb[mine, :] = gather_back(0, ret, (high, low))
    send(cb.at[mine], cb.at[mine], pair_send.at[4], pair_recv.at[4], peer)
    wait(og.at[mine], local_sem.at[2])
    wait(og.at[mine], pair_recv.at[2])
    wait(cb.at[mine], pair_recv.at[4])

    wide = latent // CORES
    cols = pl.ds(pl.multiple_of(c * wide, LANES), wide)
    columns = cb[:, cols]
    own_sum = None
    for dx in (1, xs - 1) + tuple(range(2, xs - 1)) + (0,):
        to = (x + dx) % xs
        value = dot(og[:, pl.ds(pl.multiple_of(to * block, LANES), block)], columns, 0, 0)
        if dx:
            term[dx] = value.astype(BF16)
            send(term.at[dx], rx.at[dx], gx_send, gx_recv.at[dx], me.at(x=to))
        else:
            term[dx] = value.astype(BF16)

    grad = gather_back(1, ret2, (pick,))

    @pl.when(c == 0)
    def _():
        wait(wd, local_sem.at[1])

    @pl.when(c == 1)
    def _():
        wait(wd, pair_recv.at[3])

    for xb in range(xs):
        span = pl.ds(xb * block, block)
        in_grad[:, span] = sum(
            dot(grad[:, col * LANES : (col + 1) * LANES], wd[col, span], 1, 1) for col in range(ys)
        ).astype(BF16)

    total = term[0].astype(F32)
    for dx in range(1, xs):
        wait(rx.at[dx], gx_recv.at[dx])
        total = total + rx[dx].astype(F32)
    s1[...] = total.reshape(zs // ys, ys, shard_rows, wide).astype(BF16)

    for dy in range(1, ys):
        to = (y + dy) % ys
        for q in range(zs // ys):
            send(s1.at[q, to], ry.at[dy, q], gy_send, gy_recv.at[dy], me.at(y=to))
    total = s1[:, y].astype(F32)
    for dy in range(1, ys):
        wait(ry.at[dy], gy_recv.at[dy])
        total = total + ry[dy].astype(F32)
    s2[...] = total.astype(BF16)

    owner = z % ys == y
    for q in range(zs // ys):
        to = q * ys + y

        @pl.when(to != z)
        def _():
            send(s2.at[q], rz.at[z], gz_send, gz_recv, me.at(z=to))

        @pl.when(to == z)
        def _():
            rz[z] = s2[q]

    @pl.when(owner)
    def _():
        wait(rz.at[pl.ds(0, zs - 1)], gz_recv)
        total = rz[0].astype(F32)
        for source in range(1, zs):
            total = total + rz[source].astype(F32)
        up_grad[:, cols] = total * scale
        for dy in range(ys):
            for dc in range(CORES):
                if dy or dc:
                    send(
                        up_grad.at[:, cols], up_grad.at[:, cols], go_send, go_recv.at[c],
                        me.at(y=(y + dy) % ys, c=(c + dc) % CORES),
                    )
        for _ in range(ys * CORES - 1):
            wait(up_grad.at[:, cols], go_send)
        wait(s2.at[pl.ds(0, zs // ys - 1)], gz_send)
        there = pl.ds(pl.multiple_of(other * wide, LANES), wide)
        wait(up_grad.at[:, there], go_recv.at[other])

    @pl.when(jnp.logical_not(owner))
    def _():
        for core in range(CORES):
            wait(up_grad.at[:, pl.ds(core * wide, wide)], go_recv.at[core])
        wait(s2, gz_send)

    weights.finish()
    wait(both.at[mine], pair_send.at[0])
    wait(og.at[mine], pair_send.at[2])
    wait(cb.at[mine], pair_send.at[4])
    wait(quarter, pair_send.at[1])

    @pl.when(c == 0)
    def _():
        wait(wd, pair_send.at[3])

    wait(others, z_send)
    wait(gates, n_send.at[0])
    wait(ids, n_send.at[1])
    wait(lc.at[0], n_send.at[2])
    wait(inbox.at[pl.ds(0, plane - 1)], s_send)
    for which, box in enumerate((ret, ret2)):
        wait(box.at[pl.ds(0, plane - 1)], r_send.at[which])
        wait(part.at[which], p_send.at[which])
    for _ in range(1, xs):
        wait(own, x_send)
    for _ in range(3 * xs):
        wait(own, y_send)
    wait(rx.at[pl.ds(1, xs - 1)], gx_send)
    wait(ry.at[pl.ds(1, ys - 1)], gy_send)


def local(
    sizes,
    tokens,
    gate_values,
    expert_ids,
    down_weight,
    up_weight,
    expert_gate,
    expert_up,
    expert_down,
    out_grad,
):
    xs, ys, zs = sizes
    experts = xs * zs
    tok, width = tokens.shape
    top = expert_ids.shape[1]
    shard_rows, latent = down_weight.shape
    hidden = expert_gate.shape[2]
    cap = max(2, 4 * tok * top // (3 * experts))
    plane = experts // SLAB
    slots = plane * cap
    total_tokens = tok * ys * CORES * experts
    block = shard_rows * zs
    wide = latent // CORES
    vmem = pl.BlockSpec(memory_space=pltpu.VMEM)
    hbm = pl.BlockSpec(memory_space=pl.ANY)
    dma = pltpu.SemaphoreType.DMA

    def held(*shape, kind=BF16):
        return pltpu.VMEM(shape, kind)

    return pl.pallas_call(
        functools.partial(layer_kernel, sizes, cap, 1.0 / math.sqrt(total_tokens)),
        out_shape=(
            jax.ShapeDtypeStruct((tok, width), BF16),
            jax.ShapeDtypeStruct((shard_rows, latent), F32),
        ),
        in_specs=[hbm, hbm, vmem, vmem, vmem, vmem, hbm, hbm, hbm],
        out_specs=(vmem, vmem),
        scratch_shapes=[
            held(shard_rows, latent),
            held(ys, width, LANES),
            held(ys, width, LANES),
            held(CORES * tok, width),
            held(CORES * tok, width),
            held(ys, CORES * tok, LANES),
            held(SLAB, tok, 2 * latent),
            held(SLAB, tok, top, kind=F32),
            held(SLAB, tok, top, kind=jnp.int32),
            held(SLAB, tok, slots),
            held(SLAB, tok, slots),
            held(SLAB, tok, slots),
            held(SLAB, plane, cap, 2 * latent),
            held(plane, SLAB, cap, 2 * latent),
            held(latent, hidden),
            held(latent, hidden),
            held(hidden, latent),
            held(SLAB * slots, hidden, kind=F32),
            held(SLAB * slots, hidden, kind=F32),
            held(plane, SLAB, cap, latent),
            held(plane, SLAB, cap, latent),
            held(plane, SLAB, cap, latent),
            held(plane, SLAB, cap, latent),
            held(2, tok, latent),
            held(2, tok, latent),
            held(CORES * tok, latent),
            held(xs, block, wide),
            held(xs, block, wide),
            held(zs // ys, ys, shard_rows, wide),
            held(ys, zs // ys, shard_rows, wide),
            held(zs // ys, shard_rows, wide),
            held(zs, shard_rows, wide),
            dma((3,)), dma((5,)), dma((5,)), dma(()), dma(()), dma(()), dma((xs,)),
            dma(()), dma((2, xs)), dma((xs,)), dma(()), dma((3 * CHUNKS,)),
            dma((3,)), dma((3,)), dma(()), dma(()), dma((2,)), dma((2,)), dma((2,)), dma((2,)),
            dma(()), dma((xs,)), dma(()), dma((ys,)), dma(()), dma(()), dma(()), dma((CORES,)),
        ],
        compiler_params=pltpu.CompilerParams(has_side_effects=True, vmem_limit_bytes=56 * 2**20),
        name="layer",
    )(tokens, out_grad, gate_values, expert_ids, down_weight, up_weight, expert_gate, expert_up, expert_down)


def solution(mesh):
    dp, ex = mesh.shape["dp"], mesh.shape["expert"]
    ys = dp // CORES
    sizes = (ys, ys, ex // ys)
    return jax.shard_map(
        functools.partial(local, sizes),
        mesh=mesh,
        in_specs=(
            P(("dp", "expert"), None),
            P(("dp", "expert"), None),
            P(("dp", "expert"), None),
            P("expert", None),
            P("expert", None),
            P("expert", None, None),
            P("expert", None, None),
            P("expert", None, None),
            P(("dp", "expert"), None),
        ),
        out_specs=(P(("dp", "expert"), None), P("expert", None)),
        check_vma=False,
    )
```

```python
import functools
import math

import jax
import jax.numpy as jnp
from jax import lax
from jax.experimental import pallas as pl
from jax.experimental.pallas import tpu as pltpu
from jax.sharding import PartitionSpec as P

CORES = 2
SLAB = 2
LANES = 128
CHUNKS = 8
LAG = 2
S0 = 3
S1 = 1
S2 = 1
S3 = 2
BATCH = 8
WINDOW = 2
AHEAD = 3
F32 = jnp.float32
BF16 = jnp.bfloat16


class Place:
    def __init__(self, sizes):
        self.xs, self.ys, self.zs = sizes
        dp, ex = lax.axis_index("dp"), lax.axis_index("expert")
        self.y, self.c = dp // CORES, dp % CORES
        self.x, self.z = ex // self.zs, ex % self.zs
        self.half = self.z % SLAB
        self.index = (self.x * self.ys + self.y) * CORES + self.c
        self.plane = self.xs * self.ys * CORES

    def at(self, x=None, y=None, z=None, c=None):
        x = self.x if x is None else x
        y = self.y if y is None else y
        z = self.z if z is None else z
        c = self.c if c is None else c
        return (y * CORES + c, x * self.zs + z)

    def in_plane(self, index, z=None):
        c, y, x = index % CORES, index // CORES % self.ys, index // (CORES * self.ys)
        return self.at(x=x, y=y, z=z, c=c)


def send(src, dst, send_sem, recv_sem, device):
    pltpu.make_async_remote_copy(
        src_ref=src,
        dst_ref=dst,
        send_sem=send_sem,
        recv_sem=recv_sem,
        device_id=device,
        device_id_type=pl.DeviceIdType.MESH,
    ).start()


def wait(ref, sem):
    pltpu.make_async_copy(ref, ref, sem).wait()


def rows(start, size):
    return pl.ds(pl.multiple_of(start, size), size)


def dot(left, right, left_axis=1, right_axis=0):
    return lax.dot_general(
        left, right, (((left_axis,), (right_axis,)), ((), ())), preferred_element_type=F32
    )


class Weights:
    def __init__(self, me, pairs, own_sem, send_sem, recv_sem):
        self.me, self.pairs = me, pairs
        self.own_sem, self.send_sem, self.recv_sem = own_sem, send_sem, recv_sem
        zs = me.zs
        base = me.z + zs - me.y - zs // (CORES * SLAB) * me.c
        which = base % zs // (zs // SLAB)
        away = (base + zs - (zs // SLAB) * me.half) % zs
        self.owns = base % (zs // SLAB) == 0
        self.same = jnp.logical_and(self.owns, which == me.half)
        self.first = jnp.where(which == me.half, 2, 1)
        up = jnp.logical_and(away > 0, away + 2 <= zs // 2)
        self.passes = jnp.logical_or(up, away > zs // 2 + 2)
        self.hop = (jnp.where(up, away, zs - away) + 1) // 2
        self.hops = zs // 4 - 1
        self.next = me.at(z=(me.z + jnp.where(up, 2, zs - 2)) % zs)
        self.total = CHUNKS * len(pairs)
        self.begun = self.arrived = self.point = 0
        self.passed = [0] * self.hops
        self.begin(WINDOW)

    def piece(self, i):
        src, dst = self.pairs[i // CHUNKS]
        size = dst.shape[0] // CHUNKS
        part = pl.ds(i % CHUNKS * size, size)
        return src.at[0, part], dst.at[part]

    def begin(self, upto):
        me = self.me
        upto = min(upto, self.total)
        todo = range(self.begun, upto)
        self.begun = max(self.begun, upto)
        if not todo:
            return

        @pl.when(self.same)
        def _():
            for i in todo:
                src, dst = self.piece(i)
                pltpu.make_async_copy(src, dst, self.recv_sem.at[i]).start()

        @pl.when(self.owns)
        def _():
            for i in todo:
                src, dst = self.piece(i)
                for way, ahead in enumerate((self.first, me.zs - self.first)):
                    sent = self.own_sem.at[i % WINDOW, way]
                    if i >= WINDOW:
                        wait(self.piece(i - WINDOW)[1], sent)
                    send(src, dst, sent, self.recv_sem.at[i], me.at(z=(me.z + ahead) % me.zs))

    def hand_on(self, number, upto):
        todo = range(self.passed[number], min(upto, self.total))
        self.passed[number] = max(self.passed[number], min(upto, self.total))
        if not todo:
            return

        @pl.when(jnp.logical_and(self.passes, self.hop == number + 1))
        def _():
            for i in todo:
                dst = self.piece(i)[1]
                wait(dst, self.recv_sem.at[i])
                send(dst, dst, self.send_sem, self.recv_sem.at[i], self.next)

    def step(self, count=1):
        self.point += count
        self.begin(self.point + AHEAD)
        for number in range(self.hops):
            self.hand_on(number, self.point - LAG * number)

    def arrive(self, matrices=None):
        upto = CHUNKS * (matrices or len(self.pairs))
        self.begin(upto + AHEAD)
        for number in range(self.hops):
            self.hand_on(number, upto)
        self.point = max(self.point, upto)
        todo = range(self.arrived, upto)
        self.arrived = upto

        @pl.when(jnp.logical_not(self.passes))
        def _():
            for i in todo:
                wait(self.piece(i)[1], self.recv_sem.at[i])

    def finish(self):
        @pl.when(self.owns)
        def _():
            for i in range(self.total - WINDOW, self.total):
                for way in range(2):
                    wait(self.piece(i)[1], self.own_sem.at[i % WINDOW, way])

        @pl.when(self.passes)
        def _():
            for _, dst in self.pairs:
                wait(dst, self.send_sem)


def layer_kernel(
    sizes, cap, scale,
    tokens, out_grad, gates, ids, down, up, w_gate, w_up, w_down,
    in_grad, up_grad,
    w4, wd, both, og, ogt, res, lc, gate2, ids2, pick, high, low, outbox, inbox, wg, wu, wn,
    gate_pre, up_pre, hid, result, back, ret, ret2, cb,
    term_x, term_y, rx1, ry1, sum_x, sum_y, rx2, ry2, s2, rz,
    local_sem, pair_send, pair_recv, z_send, z_recv, g_send, ax_recv, by_recv, ay_recv, bx_recv, w_own, w_send, w_recv,
    n_send, n_recv, s_send, s_recv, r_send, r_recv,
    u_send, ux1_recv, uy1_recv, ux2_recv, uy2_recv, uz_send, uz_recv, uo_send, uo_recv,
):
    me = Place(sizes)
    xs, ys, zs = sizes
    x, y, z, c, half = me.x, me.y, me.z, me.c, me.half
    other = 1 - c
    shard_rows, latent = down.shape
    tok, width = tokens.shape
    block = shard_rows * zs
    sub = block // 2
    peer = me.at(c=other)
    partner_z = z + 1 - 2 * half
    partner = me.at(z=partner_z)
    plane = me.plane
    top = ids.shape[0]
    mine = rows(c * tok, tok)
    near_x = (1, xs - 1) + tuple(range(2, xs - 1))
    near_y = (1, ys - 1) + tuple(range(2, ys - 1))
    due = {}

    def take(*names):
        for name in names:
            due.pop(name)()

    def owe(name, ref, sem, when=None):
        if when is None:
            due[name] = lambda: wait(ref, sem)
        else:
            due[name] = lambda: pl.when(when)(lambda: wait(ref, sem))

    barrier = pltpu.get_barrier_semaphore()

    def greet(device):
        pl.semaphore_signal(barrier, inc=1, device_id=device, device_id_type=pl.DeviceIdType.MESH)

    def greet_plane(d, _):
        greet(me.in_plane((me.index + d) % plane))
        return 0

    def greet_next(d, _):
        greet(me.in_plane(d, partner_z))
        return 0

    def greet_ring(d, _):
        to = (z + d) % zs

        @pl.when(to != partner_z)
        def _():
            greet(me.at(z=to))

        return 0

    lax.fori_loop(1, zs, greet_ring, 0)
    lax.fori_loop(1, plane, greet_plane, 0)
    lax.fori_loop(0, plane, greet_next, 0)

    @pl.when(c == 0)
    def _():
        pltpu.make_async_copy(tokens, both.at[mine], local_sem.at[0]).start()
        w4[y, rows((x * zs + z) * shard_rows, shard_rows)] = down[:, pl.ds(pl.multiple_of(y * LANES, LANES), LANES)]

    @pl.when(c == 1)
    def _():
        pltpu.make_async_copy(out_grad, both.at[mine], local_sem.at[0]).start()
        w4[y, rows((x * zs + z) * shard_rows, shard_rows)] = up[:, pl.ds(pl.multiple_of(y * LANES, LANES), LANES)]

    pltpu.make_async_copy(out_grad, og.at[mine], local_sem.at[2]).start()
    gate2[half] = gates[...]
    ids2[half] = ids[...]

    slots = plane * cap
    row = lax.broadcasted_iota(jnp.int32, (slots, 1), 0)
    seat, index = (row % cap).astype(F32), row // cap
    at_even = (
        index // (CORES * ys) * zs + index // CORES % ys + zs // (CORES * SLAB) * (index % CORES)
    )
    before = (
        lax.broadcasted_iota(jnp.int32, (tok, tok), 0) < lax.broadcasted_iota(jnp.int32, (tok, tok), 1)
    ).astype(BF16)

    def seats(table, q, which):
        expert = at_even + (zs // SLAB) * which
        named = jnp.zeros((slots, tok), F32)
        gate = jnp.zeros((slots, tok), F32)
        for k in range(top):
            hit = ids2[q, k : k + 1, :] == expert
            named = jnp.where(hit, 1.0, named)
            gate = jnp.where(hit, gate2[q, k : k + 1, :], gate)
        chosen = jnp.where(dot(named.astype(BF16), before) == seat, named, 0.0)
        gate = gate * chosen
        head = gate.astype(BF16)
        pick[table] = chosen.astype(BF16)
        high[table] = head
        low[table] = (gate - head.astype(F32)).astype(BF16)

    seats(0, half, half)

    pl.semaphore_wait(barrier, 2 * plane - 1 + zs - 2)

    piece = w4.at[y, rows((x * zs + z) * shard_rows, shard_rows)]
    for dz in range(1, zs):
        send(piece, piece, z_send, z_recv, me.at(z=(z + dz) % zs))
    others = w4.at[0, pl.ds(0, block - shard_rows)]
    owe("z_send", others, z_send)
    send(gates, gate2.at[half], n_send.at[0], n_recv.at[0], partner)
    send(ids, ids2.at[half], n_send.at[1], n_recv.at[1], partner)
    owe("gates", gates, n_send.at[0])
    owe("ids", ids, n_send.at[1])

    @pl.when(c == 0)
    def _():
        send(out_grad, both.at[mine], pair_send.at[0], pair_recv.at[0], peer)

    @pl.when(c == 1)
    def _():
        send(tokens, both.at[mine], pair_send.at[0], pair_recv.at[0], peer)

    owe("both", both.at[mine], pair_send.at[0])
    weights = Weights(me, ((w_gate, wg), (w_up, wu), (w_down, wn)), w_own, w_send, w_recv)
    send(out_grad, og.at[mine], pair_send.at[2], pair_recv.at[2], peer)
    owe("og", og.at[mine], pair_send.at[2])
    weights.step(S0)
    wait(others, z_recv)

    def first_rows(xx):
        return rows(xx * block, sub)

    def second_rows(xx):
        return rows(xx * block + sub, sub)

    def away(at, size, d):
        return (at + size - d) % size

    for dx, dy in zip(near_x, near_y):
        a, b = w4.at[y, first_rows(x)], w4.at[y, second_rows(x)]
        send(a, a, g_send, ax_recv.at[dx], me.at(x=(x + dx) % xs))
        send(b, b, g_send, by_recv.at[dy], me.at(y=(y + dy) % ys))
    for step in range(xs):
        dx, dy = ((0,) + near_x)[step], ((0,) + near_y)[step]
        a = w4.at[y, first_rows(away(x, xs, dx))]
        b = w4.at[away(y, ys, dy), second_rows(x)]
        if step:
            wait(a, ax_recv.at[dx])
            wait(b, by_recv.at[dy])
        for to_x, to_y in zip(near_x, near_y):
            send(a, a, g_send, ay_recv.at[to_y], me.at(y=(y + to_y) % ys))
            send(b, b, g_send, bx_recv.at[to_x], me.at(x=(x + to_x) % xs))
        weights.step(S1)

    def all_gathered():
        for _ in range(2 * (xs - 1)):
            wait(w4.at[0, pl.ds(0, sub)], g_send)
            wait(w4.at[0, pl.ds(0, xs * sub)], g_send)

    due["gather"] = all_gathered

    wait(gates, n_recv.at[0])
    wait(ids, n_recv.at[1])
    seats(1, 1 - half, half)
    seats(2, half, 1 - half)

    for dx, dy in zip(near_x, near_y):
        wait(w4.at[0, pl.ds(0, xs * sub)], ay_recv.at[dy])
        wait(w4.at[0, pl.ds(0, ys * sub)], bx_recv.at[dx])
        weights.step(S2)

    wait(both.at[mine], local_sem.at[0])
    wait(both.at[mine], pair_recv.at[0])

    def lanes(col):
        return pl.ds(pl.multiple_of(c * latent + col * LANES, LANES), LANES)

    for col in range(ys):
        res[col] = dot(both[...], w4[col]).astype(BF16)
        send(res.at[col, rows(other * tok, tok)], lc.at[half, :, lanes(col)], pair_send.at[1], pair_recv.at[1], peer)
    for col in range(ys):
        lc[half, :, lanes(col)] = res[col, mine, :]
    quarter = lc.at[half, :, pl.ds(0, latent)]
    owe("quarter", quarter, pair_send.at[1])

    @pl.when(c == 0)
    def _():
        send(w4, wd, pair_send.at[3], pair_recv.at[3], peer)
        pltpu.make_async_copy(w4, wd, local_sem.at[1]).start()

    owe("wd", wd, pair_send.at[3], c == 0)
    weights.step(S3)
    wait(quarter, pair_recv.at[1])
    send(lc.at[half], lc.at[half], n_send.at[2], n_recv.at[2], partner)
    owe("lc", lc.at[0], n_send.at[2])

    def dispatch(table, q):
        tile = 8

        def fill(t, _):
            span = rows(t * tile * cap, tile * cap)
            picked = dot(pick[table, span], lc[q, :, :latent])
            cot = dot(high[table, span], lc[q, :, latent:]) + dot(low[table, span], lc[q, :, latent:])
            outbox[q, pl.ds(t * tile, tile), :, :latent] = picked.astype(BF16).reshape(tile, cap, latent)
            outbox[q, pl.ds(t * tile, tile), :, latent:] = cot.astype(BF16).reshape(tile, cap, latent)
            return 0

        lax.fori_loop(0, plane // tile, fill, 0)

        def post(d, _):
            to = (me.index + d) % plane
            send(outbox.at[q, to], inbox.at[me.index, q], s_send, s_recv, me.in_plane(to))
            return 0

        for start in range(1, plane, BATCH):
            lax.fori_loop(start, min(start + BATCH, plane), post, 0)
            weights.step()
        inbox[me.index, q] = outbox[q, me.index]

    dispatch(0, half)
    wait(lc.at[0], n_recv.at[2])
    dispatch(1, 1 - half)
    owe("inbox", inbox.at[pl.ds(0, plane - 1)], s_send)
    wait(og.at[mine], local_sem.at[2])
    wait(og.at[mine], pair_recv.at[2])
    for xb in range(xs):
        ogt[pl.ds(xb * block, block), :] = og[:, pl.ds(xb * block, block)].T
        weights.step()
    weights.arrive(2)
    wait(inbox.at[pl.ds(0, plane - 1)], s_recv)

    group = 8
    size = group * SLAB * cap

    def tile_of(t):
        return (t + me.index // group) % (plane // group)

    def post_back(box, ret_box, which, g):
        def post(d, _):
            to = g * group + d

            send(
                box.at[to, 1 - half], ret_box.at[half, me.index],
                r_send.at[which, 1], r_recv.at[which, 1], me.in_plane(to, partner_z),
            )

            @pl.when(to != me.index)
            def _():
                send(
                    box.at[to, half], ret_box.at[half, me.index],
                    r_send.at[which, 0], r_recv.at[which, 0], me.in_plane(to),
                )

            @pl.when(to == me.index)
            def _():
                ret_box[half, to] = box[to, half]

            return 0

        lax.fori_loop(0, group, post, 0)

    def before_hidden(t):
        g = tile_of(t)
        box, span = pl.ds(g * group, group), rows(g * size, size)
        value = inbox[box, :, :, :latent].reshape(size, latent)
        pre = dot(value, wg[...])
        pre_up = dot(value, wu[...])
        gate_pre[span, :] = pre
        up_pre[span, :] = pre_up
        hid[span, :] = (pre * jax.nn.sigmoid(pre) * pre_up).astype(BF16)

    for t in range(plane // group):
        before_hidden(t)
        weights.step(2)
    weights.arrive()
    due["weights"] = weights.finish

    def forward(t, _):
        g = tile_of(t)
        box, span = pl.ds(g * group, group), rows(g * size, size)
        result[box] = dot(hid[span, :], wn[...]).astype(BF16).reshape(group, SLAB, cap, latent)
        post_back(result, ret, 0, g)
        return 0

    lax.fori_loop(0, plane // group, forward, 0)

    def backward(t, _):
        g = tile_of(t)
        box, span = pl.ds(g * group, group), rows(g * size, size)
        value = inbox[box, :, :, latent:].reshape(size, latent)
        hidden_cot = dot(value, wn[...], 1, 1)
        pre, pre_up = gate_pre[span, :], up_pre[span, :]
        sig = jax.nn.sigmoid(pre)
        gate_cot = (hidden_cot * pre_up * sig * (1.0 + pre * (1.0 - sig))).astype(BF16)
        up_cot = (hidden_cot * pre * sig).astype(BF16)
        total = dot(gate_cot, wg[...], 1, 1) + dot(up_cot, wu[...], 1, 1)
        back[box] = total.astype(BF16).reshape(group, SLAB, cap, latent)
        post_back(back, ret2, 1, g)
        return 0

    lax.fori_loop(0, plane // group, backward, 0)
    for which, box in enumerate((ret, ret2)):
        owe(f"back{which}", box.at[0, pl.ds(0, plane - 1)], r_send.at[which, 0])
        owe(f"next{which}", box.at[0], r_send.at[which, 1])

    def sum_back(which, box, weigh):
        wait(box.at[0, pl.ds(0, plane - 1)], r_recv.at[which, 0])
        wait(box.at[0], r_recv.at[which, 1])
        total = jnp.zeros((tok, latent), F32)
        for table, plane_half in ((0, half), (2, 1 - half)):
            value = box[plane_half].reshape(slots, latent)
            for m in weigh:
                total = total + dot(m[table], value, 0, 0)
        return total.astype(BF16)

    cb[mine, :] = sum_back(0, ret, (high, low))
    send(cb.at[mine], cb.at[mine], pair_send.at[4], pair_recv.at[4], peer)
    owe("cb", cb.at[mine], pair_send.at[4])
    wait(cb.at[mine], pair_recv.at[4])

    wide = latent // CORES
    cols = pl.ds(pl.multiple_of(c * wide, LANES), wide)
    columns = cb[:, cols]
    turns = zs // ys
    for dx in near_x + (0,):
        to = (x + dx) % xs
        value = dot(ogt[rows(to * block, block), :], columns).astype(BF16)
        term_x[dx] = value[:, :LANES]
        if dx:
            send(term_x.at[dx], rx1.at[dx], u_send, ux1_recv.at[dx], me.at(x=to))
        second = value[:, LANES:].reshape(turns, ys, shard_rows, LANES)
        for yy in range(ys):
            term_y[yy, to] = second[:, yy]
    for dy in near_y:
        to = (y + dy) % ys
        send(term_y.at[to], ry1.at[dy], u_send, uy1_recv.at[dy], me.at(y=to))

    total = term_x[0].astype(F32)
    for dx in near_x:
        wait(rx1.at[dx], ux1_recv.at[dx])
        total = total + rx1[dx].astype(F32)
    total = total.astype(BF16).reshape(turns, ys, shard_rows, LANES)
    for yy in range(ys):
        sum_x[yy] = total[:, yy]
    for dy in near_y:
        to = (y + dy) % ys
        send(sum_x.at[to], ry2.at[dy], u_send, uy2_recv.at[dy], me.at(y=to))
    total = term_y[y].astype(F32)
    for dy in near_y:
        wait(ry1.at[dy], uy1_recv.at[dy])
        total = total + ry1[dy].astype(F32)
    sum_y[...] = total.astype(BF16)
    for dx in near_x:
        to = (x + dx) % xs
        send(sum_y.at[to], rx2.at[dx], u_send, ux2_recv.at[dx], me.at(x=to))

    grad = sum_back(1, ret2, (pick,))

    @pl.when(c == 0)
    def _():
        wait(wd, local_sem.at[1])

    @pl.when(c == 1)
    def _():
        wait(wd, pair_recv.at[3])

    def in_rows(xb):
        span = pl.ds(xb * block, block)
        in_grad[:, span] = sum(
            dot(grad[:, col * LANES : (col + 1) * LANES], wd[col, span], 1, 1) for col in range(ys)
        ).astype(BF16)

    for xb in range(xs):
        in_rows(xb)

    total = sum_x[y].astype(F32)
    for dy in near_y:
        wait(ry2.at[dy], uy2_recv.at[dy])
        total = total + ry2[dy].astype(F32)
    s2[:, :, :LANES] = total.astype(BF16)
    total = sum_y[x].astype(F32)
    for dx in near_x:
        wait(rx2.at[dx], ux2_recv.at[dx])
        total = total + rx2[dx].astype(F32)
    s2[:, :, LANES:] = total.astype(BF16)

    def up_grad_sent():
        for _ in near_x:
            wait(term_x.at[0], u_send)
            wait(term_y.at[0], u_send)
            wait(sum_x.at[0], u_send)
            wait(sum_y.at[0], u_send)

    due["up_grad"] = up_grad_sent

    owner = z % ys == y
    for q in range(turns):
        to = q * ys + y

        @pl.when(to != z)
        def _():
            send(s2.at[q], rz.at[z], uz_send, uz_recv, me.at(z=to))

        @pl.when(to == z)
        def _():
            rz[z] = s2[q]

    @pl.when(owner)
    def _():
        wait(rz.at[pl.ds(0, zs - 1)], uz_recv)
        total = rz[0].astype(F32)
        for source in range(1, zs):
            total = total + rz[source].astype(F32)
        up_grad[:, cols] = total * scale
        for dy in range(ys):
            for dc in range(CORES):
                if dy or dc:
                    send(
                        up_grad.at[:, cols], up_grad.at[:, cols], uo_send, uo_recv.at[c],
                        me.at(y=(y + dy) % ys, c=(c + dc) % CORES),
                    )
        for _ in range(ys * CORES - 1):
            wait(up_grad.at[:, cols], uo_send)
        wait(s2.at[pl.ds(0, turns - 1)], uz_send)
        there = pl.ds(pl.multiple_of(other * wide, LANES), wide)
        wait(up_grad.at[:, there], uo_recv.at[other])

    @pl.when(jnp.logical_not(owner))
    def _():
        for core in range(CORES):
            wait(up_grad.at[:, pl.ds(core * wide, wide)], uo_recv.at[core])
        wait(s2, uz_send)

    take(*list(due))


def local(
    sizes,
    tokens,
    gate_values,
    expert_ids,
    down_weight,
    up_weight,
    expert_gate,
    expert_up,
    expert_down,
    out_grad,
):
    xs, ys, zs = sizes
    experts = xs * zs
    tok, width = tokens.shape
    top = expert_ids.shape[1]
    turns = zs // ys
    shard_rows, latent = down_weight.shape
    hidden = expert_gate.shape[2]
    cap = max(2, 4 * tok * top // (3 * experts))
    plane = experts // SLAB
    slots = plane * cap
    total_tokens = tok * ys * CORES * experts
    block = shard_rows * zs
    wide = latent // CORES
    vmem = pl.BlockSpec(memory_space=pltpu.VMEM)
    hbm = pl.BlockSpec(memory_space=pl.ANY)
    dma = pltpu.SemaphoreType.DMA

    def held(*shape, kind=BF16):
        return pltpu.VMEM(shape, kind)

    return pl.pallas_call(
        functools.partial(layer_kernel, sizes, cap, 1.0 / math.sqrt(total_tokens)),
        out_shape=(
            jax.ShapeDtypeStruct((tok, width), BF16),
            jax.ShapeDtypeStruct((shard_rows, latent), F32),
        ),
        in_specs=[hbm, hbm, vmem, vmem, vmem, vmem, hbm, hbm, hbm],
        out_specs=(vmem, vmem),
        scratch_shapes=[
            held(ys, width, LANES),
            held(ys, width, LANES),
            held(CORES * tok, width),
            held(CORES * tok, width),
            held(width, CORES * tok),
            held(ys, CORES * tok, LANES),
            held(SLAB, tok, 2 * latent),
            held(SLAB, top, tok, kind=F32),
            held(SLAB, top, tok, kind=jnp.int32),
            held(SLAB + 1, slots, tok),
            held(SLAB + 1, slots, tok),
            held(SLAB + 1, slots, tok),
            held(SLAB, plane, cap, 2 * latent),
            held(plane, SLAB, cap, 2 * latent),
            held(latent, hidden),
            held(latent, hidden),
            held(hidden, latent),
            held(SLAB * slots, hidden, kind=F32),
            held(SLAB * slots, hidden, kind=F32),
            held(SLAB * slots, hidden),
            held(plane, SLAB, cap, latent),
            held(plane, SLAB, cap, latent),
            held(SLAB, plane, cap, latent),
            held(SLAB, plane, cap, latent),
            held(CORES * tok, latent),
            held(xs, block, LANES),
            held(ys, xs, turns, shard_rows, LANES),
            held(xs, block, LANES),
            held(ys, xs, turns, shard_rows, LANES),
            held(ys, turns, shard_rows, LANES),
            held(xs, turns, shard_rows, LANES),
            held(xs, turns, shard_rows, LANES),
            held(ys, turns, shard_rows, LANES),
            held(turns, shard_rows, wide),
            held(zs, shard_rows, wide),
            dma((3,)), dma((5,)), dma((5,)), dma(()), dma(()),
            dma(()), dma((xs,)), dma((ys,)), dma((ys,)), dma((xs,)), dma((WINDOW, 2)), dma(()), dma((3 * CHUNKS,)),
            dma((3,)), dma((3,)), dma(()), dma(()), dma((2, 2)), dma((2, 2)),
            dma(()), dma((xs,)), dma((ys,)), dma((xs,)), dma((ys,)), dma(()), dma(()), dma(()), dma((CORES,)),
        ],
        compiler_params=pltpu.CompilerParams(
            has_side_effects=True, collective_id=0, vmem_limit_bytes=56 * 2**20
        ),
        name="layer",
    )(tokens, out_grad, gate_values.T, expert_ids.T, down_weight, up_weight, expert_gate, expert_up, expert_down)


def solution(mesh):
    dp, ex = mesh.shape["dp"], mesh.shape["expert"]
    ys = dp // CORES
    sizes = (ys, ys, ex // ys)
    return jax.shard_map(
        functools.partial(local, sizes),
        mesh=mesh,
        in_specs=(
            P(("dp", "expert"), None),
            P(("dp", "expert"), None),
            P(("dp", "expert"), None),
            P("expert", None),
            P("expert", None),
            P("expert", None, None),
            P("expert", None, None),
            P("expert", None, None),
            P(("dp", "expert"), None),
        ),
        out_specs=(P(("dp", "expert"), None), P("expert", None)),
        check_vma=False,
    )
```

```python
import functools
import math

import jax
import jax.numpy as jnp
from jax import lax
from jax.experimental import pallas as pl
from jax.experimental.pallas import tpu as pltpu
from jax.sharding import PartitionSpec as P

CORES = 2
SLAB = 2
LANES = 128
CHUNKS = 8
LAST = 16
LAG = 2
IN_RING = 3
IN_PLANE = 1
IN_WAIT = 1
IN_PRODUCT = 2
BATCH = 16
WINDOW = 2
AHEAD = 3
F32 = jnp.float32
BF16 = jnp.bfloat16


class Place:
    def __init__(self, sizes):
        self.xs, self.ys, self.zs = sizes
        dp, ex = lax.axis_index("dp"), lax.axis_index("expert")
        self.y, self.c = dp // CORES, dp % CORES
        self.x, self.z = ex // self.zs, ex % self.zs
        self.half = self.z % SLAB
        self.index = (self.x * self.ys + self.y) * CORES + self.c
        self.plane = self.xs * self.ys * CORES

    def at(self, x=None, y=None, z=None, c=None):
        x = self.x if x is None else x
        y = self.y if y is None else y
        z = self.z if z is None else z
        c = self.c if c is None else c
        return (y * CORES + c, x * self.zs + z)

    def in_plane(self, index, z=None):
        c, y, x = index % CORES, index // CORES % self.ys, index // (CORES * self.ys)
        return self.at(x=x, y=y, z=z, c=c)


def send(src, dst, send_sem, recv_sem, device):
    pltpu.make_async_remote_copy(
        src_ref=src,
        dst_ref=dst,
        send_sem=send_sem,
        recv_sem=recv_sem,
        device_id=device,
        device_id_type=pl.DeviceIdType.MESH,
    ).start()


def wait(ref, sem):
    pltpu.make_async_copy(ref, ref, sem).wait()


def rows(start, size):
    return pl.ds(pl.multiple_of(start, size), size)


def dot(left, right, left_axis=1, right_axis=0):
    return lax.dot_general(
        left, right, (((left_axis,), (right_axis,)), ((), ())), preferred_element_type=F32
    )


class Weights:
    def __init__(self, me, pairs, own_sem, send_sem, recv_sem):
        self.me, self.pairs = me, pairs
        self.own_sem, self.send_sem, self.recv_sem = own_sem, send_sem, recv_sem
        zs = me.zs
        base = me.z + zs - me.y - zs // (CORES * SLAB) * me.c
        which = base % zs // (zs // SLAB)
        away = (base + zs - (zs // SLAB) * me.half) % zs
        self.owns = base % (zs // SLAB) == 0
        self.same = jnp.logical_and(self.owns, which == me.half)
        self.first = jnp.where(which == me.half, 2, 1)
        up = jnp.logical_and(away > 0, away + 2 <= zs // 2)
        self.passes = jnp.logical_or(up, away > zs // 2 + 2)
        self.hop = (jnp.where(up, away, zs - away) + 1) // 2
        self.hops = zs // 4 - 1
        self.next = me.at(z=(me.z + jnp.where(up, 2, zs - 2)) % zs)
        self.counts = (CHUNKS, CHUNKS, LAST)
        self.total = sum(self.counts)
        self.begun = self.arrived = self.point = 0
        self.passed = [0] * self.hops
        self.begin(WINDOW)

    def piece(self, i):
        matrix = 0
        while i >= self.counts[matrix]:
            i -= self.counts[matrix]
            matrix += 1
        src, dst = self.pairs[matrix]
        size = dst.shape[0] // self.counts[matrix]
        part = pl.ds(i * size, size)
        return src.at[0, part], dst.at[part]

    def begin(self, upto):
        me = self.me
        upto = min(upto, self.total)
        todo = range(self.begun, upto)
        self.begun = max(self.begun, upto)
        if not todo:
            return

        @pl.when(self.same)
        def _():
            for i in todo:
                src, dst = self.piece(i)
                pltpu.make_async_copy(src, dst, self.recv_sem.at[i]).start()

        @pl.when(self.owns)
        def _():
            for i in todo:
                src, dst = self.piece(i)
                for way, ahead in enumerate((self.first, me.zs - self.first)):
                    sent = self.own_sem.at[i % WINDOW, way]
                    if i >= WINDOW:
                        wait(self.piece(i - WINDOW)[1], sent)
                    send(src, dst, sent, self.recv_sem.at[i], me.at(z=(me.z + ahead) % me.zs))

    def hand_on(self, number, upto):
        todo = range(self.passed[number], min(upto, self.total))
        self.passed[number] = max(self.passed[number], min(upto, self.total))
        if not todo:
            return

        @pl.when(jnp.logical_and(self.passes, self.hop == number + 1))
        def _():
            for i in todo:
                dst = self.piece(i)[1]
                wait(dst, self.recv_sem.at[i])
                send(dst, dst, self.send_sem, self.recv_sem.at[i], self.next)

    def step(self, count=1):
        self.point += count
        self.begin(self.point + AHEAD)
        for number in range(self.hops):
            self.hand_on(number, self.point - LAG * number)

    def arrive(self, matrices=None):
        upto = sum(self.counts[:matrices])
        self.begin(upto + AHEAD)
        for number in range(self.hops):
            self.hand_on(number, upto)
        self.point = max(self.point, upto)
        todo = range(self.arrived, upto)
        self.arrived = upto

        @pl.when(jnp.logical_not(self.passes))
        def _():
            for i in todo:
                wait(self.piece(i)[1], self.recv_sem.at[i])

    def finish(self):
        @pl.when(self.owns)
        def _():
            for i in range(self.total - WINDOW, self.total):
                for way in range(2):
                    wait(self.piece(i)[1], self.own_sem.at[i % WINDOW, way])

        @pl.when(self.passes)
        def _():
            for _, dst in self.pairs:
                wait(dst, self.send_sem)


def layer_kernel(
    sizes, cap, scale,
    tokens, out_grad, gates, ids, down, up, w_gate, w_up, w_down,
    in_grad, up_grad,
    w4, wd, both, og, ogt, res, lc, gate2, ids2, pick, high, low, outbox, inbox, wg, wu, wn,
    gate_pre, up_pre, hid, result, back, ret, ret2, cb,
    term_x, term_y, rx1, ry1, sum_x, sum_y, rx2, ry2, s2, rz, shared,
    local_sem, pair_send, pair_recv, z_send, z_recv, g_send, ax_recv, by_recv, ay_recv, bx_recv, w_own, w_send, w_recv,
    n_send, n_recv, s_send, s_recv, r_send, r_recv,
    u_send, ux1_recv, uy1_recv, ux2_recv, uy2_recv, uz_send, uz_recv, uo_send, uo_recv,
):
    me = Place(sizes)
    xs, ys, zs = sizes
    x, y, z, c, half = me.x, me.y, me.z, me.c, me.half
    other = 1 - c
    shard_rows, latent = down.shape
    tok, width = tokens.shape
    block = shard_rows * zs
    sub = block // 2
    peer = me.at(c=other)
    partner_z = z + 1 - 2 * half
    partner = me.at(z=partner_z)
    plane = me.plane
    top = ids.shape[0]
    mine = rows(c * tok, tok)
    near_x = (1, xs - 1) + tuple(range(2, xs - 1))
    near_y = (1, ys - 1) + tuple(range(2, ys - 1))
    due = {}

    def take(*names):
        for name in names:
            due.pop(name)()

    def owe(name, ref, sem, when=None):
        if when is None:
            due[name] = lambda: wait(ref, sem)
        else:
            due[name] = lambda: pl.when(when)(lambda: wait(ref, sem))

    barrier = pltpu.get_barrier_semaphore()

    def greet(device):
        pl.semaphore_signal(barrier, inc=1, device_id=device, device_id_type=pl.DeviceIdType.MESH)

    def greet_plane(d, _):
        greet(me.in_plane((me.index + d) % plane))
        return 0

    def greet_next(d, _):
        greet(me.in_plane(d, partner_z))
        return 0

    def greet_ring(d, _):
        to = (z + d) % zs

        @pl.when(to != partner_z)
        def _():
            greet(me.at(z=to))

        return 0

    lax.fori_loop(1, zs, greet_ring, 0)
    lax.fori_loop(1, plane, greet_plane, 0)
    lax.fori_loop(0, plane, greet_next, 0)

    @pl.when(c == 0)
    def _():
        pltpu.make_async_copy(tokens, both.at[mine], local_sem.at[0]).start()
        w4[y, rows((x * zs + z) * shard_rows, shard_rows)] = down[:, pl.ds(pl.multiple_of(y * LANES, LANES), LANES)]

    @pl.when(c == 1)
    def _():
        pltpu.make_async_copy(out_grad, both.at[mine], local_sem.at[0]).start()
        w4[y, rows((x * zs + z) * shard_rows, shard_rows)] = up[:, pl.ds(pl.multiple_of(y * LANES, LANES), LANES)]

    pltpu.make_async_copy(out_grad, og.at[mine], local_sem.at[2]).start()
    gate2[half] = gates[...]
    ids2[half] = ids[...]

    slots = plane * cap
    row = lax.broadcasted_iota(jnp.int32, (slots, 1), 0)
    seat, index = (row % cap).astype(F32), row // cap
    at_even = (
        index // (CORES * ys) * zs + index // CORES % ys + zs // (CORES * SLAB) * (index % CORES)
    )
    before = (
        lax.broadcasted_iota(jnp.int32, (tok, tok), 0) < lax.broadcasted_iota(jnp.int32, (tok, tok), 1)
    ).astype(BF16)

    def seats(table, q, which):
        expert = at_even + (zs // SLAB) * which
        named = jnp.zeros((slots, tok), F32)
        gate = jnp.zeros((slots, tok), F32)
        for k in range(top):
            hit = ids2[q, k : k + 1, :] == expert
            named = jnp.where(hit, 1.0, named)
            gate = jnp.where(hit, gate2[q, k : k + 1, :], gate)
        chosen = jnp.where(dot(named.astype(BF16), before) == seat, named, 0.0)
        gate = gate * chosen
        head = gate.astype(BF16)
        pick[table] = chosen.astype(BF16)
        high[table] = head
        low[table] = (gate - head.astype(F32)).astype(BF16)

    seats(0, half, half)

    pl.semaphore_wait(barrier, 2 * plane - 1 + zs - 2)

    piece = w4.at[y, rows((x * zs + z) * shard_rows, shard_rows)]
    for dz in range(1, zs):
        send(piece, piece, z_send, z_recv, me.at(z=(z + dz) % zs))
    others = w4.at[0, pl.ds(0, block - shard_rows)]
    owe("z_send", others, z_send)
    send(gates, gate2.at[half], n_send.at[0], n_recv.at[0], partner)
    send(ids, ids2.at[half], n_send.at[1], n_recv.at[1], partner)
    owe("gates", gates, n_send.at[0])
    owe("ids", ids, n_send.at[1])

    @pl.when(c == 0)
    def _():
        send(out_grad, both.at[mine], pair_send.at[0], pair_recv.at[0], peer)

    @pl.when(c == 1)
    def _():
        send(tokens, both.at[mine], pair_send.at[0], pair_recv.at[0], peer)

    owe("both", both.at[mine], pair_send.at[0])
    weights = Weights(me, ((w_gate, wg), (w_up, wu), (w_down, wn)), w_own, w_send, w_recv)
    send(out_grad, og.at[mine], pair_send.at[2], pair_recv.at[2], peer)
    owe("og", og.at[mine], pair_send.at[2])
    weights.step(IN_RING)
    wait(others, z_recv)

    def first_rows(xx):
        return rows(xx * block, sub)

    def second_rows(xx):
        return rows(xx * block + sub, sub)

    def away(at, size, d):
        return (at + size - d) % size

    for dx, dy in zip(near_x, near_y):
        a, b = w4.at[y, first_rows(x)], w4.at[y, second_rows(x)]
        send(a, a, g_send, ax_recv.at[dx], me.at(x=(x + dx) % xs))
        send(b, b, g_send, by_recv.at[dy], me.at(y=(y + dy) % ys))
    for step in range(xs):
        dx, dy = ((0,) + near_x)[step], ((0,) + near_y)[step]
        a = w4.at[y, first_rows(away(x, xs, dx))]
        b = w4.at[away(y, ys, dy), second_rows(x)]
        if step:
            wait(a, ax_recv.at[dx])
            wait(b, by_recv.at[dy])
        for to_x, to_y in zip(near_x, near_y):
            send(a, a, g_send, ay_recv.at[to_y], me.at(y=(y + to_y) % ys))
            send(b, b, g_send, bx_recv.at[to_x], me.at(x=(x + to_x) % xs))
        weights.step(IN_PLANE)

    def all_gathered():
        for _ in range(2 * (xs - 1)):
            wait(w4.at[0, pl.ds(0, sub)], g_send)
            wait(w4.at[0, pl.ds(0, xs * sub)], g_send)

    due["gather"] = all_gathered

    wait(gates, n_recv.at[0])
    wait(ids, n_recv.at[1])
    seats(1, 1 - half, half)
    seats(2, half, 1 - half)

    for dx, dy in zip(near_x, near_y):
        wait(w4.at[0, pl.ds(0, xs * sub)], ay_recv.at[dy])
        wait(w4.at[0, pl.ds(0, ys * sub)], bx_recv.at[dx])
        weights.step(IN_WAIT)

    wait(both.at[mine], local_sem.at[0])
    wait(both.at[mine], pair_recv.at[0])

    def lanes(col):
        return pl.ds(pl.multiple_of(c * latent + col * LANES, LANES), LANES)

    for col in range(ys):
        res[col] = dot(both[...], w4[col]).astype(BF16)
        theirs, place = res.at[col, rows(other * tok, tok)], lc.at[half, :, lanes(col)]
        send(res.at[col, mine], place, n_send.at[2], n_recv.at[2], partner)
        send(theirs, place, n_send.at[2], n_recv.at[2], me.at(z=partner_z, c=other))
        send(theirs, place, pair_send.at[1], pair_recv.at[1], peer)
    for col in range(ys):
        lc[half, :, lanes(col)] = res[col, mine, :]
    quarter = lc.at[half, :, pl.ds(0, latent)]
    owe("quarter", quarter, pair_send.at[1])

    @pl.when(c == 0)
    def _():
        send(w4, wd, pair_send.at[3], pair_recv.at[3], peer)
        pltpu.make_async_copy(w4, wd, local_sem.at[1]).start()

    owe("wd", wd, pair_send.at[3], c == 0)
    weights.step(IN_PRODUCT)
    wait(quarter, pair_recv.at[1])
    owe("lc", lc.at[0], n_send.at[2])

    def dispatch(table, q):
        tile = 8

        def fill(t, _):
            span = rows(t * tile * cap, tile * cap)
            picked = dot(pick[table, span], lc[q, :, :latent])
            cot = dot(high[table, span], lc[q, :, latent:]) + dot(low[table, span], lc[q, :, latent:])
            outbox[q, pl.ds(t * tile, tile), :, :latent] = picked.astype(BF16).reshape(tile, cap, latent)
            outbox[q, pl.ds(t * tile, tile), :, latent:] = cot.astype(BF16).reshape(tile, cap, latent)
            return 0

        lax.fori_loop(0, plane // tile, fill, 0)

        def post(d, _):
            to = (me.index + d) % plane
            send(outbox.at[q, to], inbox.at[me.index, q], s_send, s_recv, me.in_plane(to))
            return 0

        for start in range(1, plane, BATCH):
            lax.fori_loop(start, min(start + BATCH, plane), post, 0)
            weights.step()
        inbox[me.index, q] = outbox[q, me.index]

    dispatch(0, half)
    wait(lc.at[0], n_recv.at[2])
    dispatch(1, 1 - half)
    owe("inbox", inbox.at[pl.ds(0, plane - 1)], s_send)
    wait(og.at[mine], local_sem.at[2])
    wait(og.at[mine], pair_recv.at[2])
    for xb in range(xs):
        ogt[pl.ds(xb * block, block), :] = og[:, pl.ds(xb * block, block)].T
        weights.step()
    weights.arrive(2)
    wait(inbox.at[pl.ds(0, plane - 1)], s_recv)

    group = 8
    size = group * SLAB * cap

    def tile_of(t):
        return (t + me.index // group) % (plane // group)

    def post_back(box, ret_box, which, g):
        def post(d, _):
            to = g * group + d

            send(
                box.at[to, 1 - half], ret_box.at[half, me.index],
                r_send.at[which, 1], r_recv.at[which, 1], me.in_plane(to, partner_z),
            )

            @pl.when(to != me.index)
            def _():
                send(
                    box.at[to, half], ret_box.at[half, me.index],
                    r_send.at[which, 0], r_recv.at[which, 0], me.in_plane(to),
                )

            @pl.when(to == me.index)
            def _():
                ret_box[half, to] = box[to, half]

            return 0

        lax.fori_loop(0, group, post, 0)

    def before_hidden(t):
        g = tile_of(t)
        box, span = pl.ds(g * group, group), rows(g * size, size)
        value = inbox[box, :, :, :latent].reshape(size, latent)
        pre = dot(value, wg[...])
        pre_up = dot(value, wu[...])
        gate_pre[span, :] = pre
        up_pre[span, :] = pre_up
        hid[span, :] = (pre * jax.nn.sigmoid(pre) * pre_up).astype(BF16)

    for t in range(plane // group):
        before_hidden(t)
        weights.step(2)
    weights.arrive()
    due["weights"] = weights.finish

    def forward(t, _):
        g = tile_of(t)
        box, span = pl.ds(g * group, group), rows(g * size, size)
        result[box] = dot(hid[span, :], wn[...]).astype(BF16).reshape(group, SLAB, cap, latent)
        post_back(result, ret, 0, g)
        return 0

    lax.fori_loop(0, plane // group, forward, 0)

    def backward(t, _):
        g = tile_of(t)
        box, span = pl.ds(g * group, group), rows(g * size, size)
        value = inbox[box, :, :, latent:].reshape(size, latent)
        hidden_cot = dot(value, wn[...], 1, 1)
        pre, pre_up = gate_pre[span, :], up_pre[span, :]
        sig = jax.nn.sigmoid(pre)
        gate_cot = (hidden_cot * pre_up * sig * (1.0 + pre * (1.0 - sig))).astype(BF16)
        up_cot = (hidden_cot * pre * sig).astype(BF16)
        total = dot(gate_cot, wg[...], 1, 1) + dot(up_cot, wu[...], 1, 1)
        back[box] = total.astype(BF16).reshape(group, SLAB, cap, latent)
        post_back(back, ret2, 1, g)
        return 0

    lax.fori_loop(0, plane // group, backward, 0)
    for which, box in enumerate((ret, ret2)):
        owe(f"back{which}", box.at[0, pl.ds(0, plane - 1)], r_send.at[which, 0])
        owe(f"next{which}", box.at[0], r_send.at[which, 1])

    def sum_back(which, box, weigh):
        wait(box.at[0, pl.ds(0, plane - 1)], r_recv.at[which, 0])
        wait(box.at[0], r_recv.at[which, 1])
        total = jnp.zeros((tok, latent), F32)
        for table, plane_half in ((0, half), (2, 1 - half)):
            value = box[plane_half].reshape(slots, latent)
            for m in weigh:
                total = total + dot(m[table], value, 0, 0)
        return total.astype(BF16)

    cb[mine, :] = sum_back(0, ret, (high, low))
    send(cb.at[mine], cb.at[mine], pair_send.at[4], pair_recv.at[4], peer)
    owe("cb", cb.at[mine], pair_send.at[4])
    wait(cb.at[mine], pair_recv.at[4])

    wide = latent // CORES
    cols = pl.ds(pl.multiple_of(c * wide, LANES), wide)
    columns = cb[:, cols]
    turns = zs // ys
    for dx in near_x + (0,):
        to = (x + dx) % xs
        value = dot(ogt[rows(to * block, block), :], columns).astype(BF16)
        term_x[dx] = value[:, :LANES]
        if dx:
            send(term_x.at[dx], rx1.at[dx], u_send, ux1_recv.at[dx], me.at(x=to))
        second = value[:, LANES:].reshape(turns, ys, shard_rows, LANES)
        for yy in range(ys):
            term_y[yy, to] = second[:, yy]
    for dy in near_y:
        to = (y + dy) % ys
        send(term_y.at[to], ry1.at[dy], u_send, uy1_recv.at[dy], me.at(y=to))

    grad = sum_back(1, ret2, (pick,))
    total = term_x[0].astype(F32)
    for dx in near_x:
        wait(rx1.at[dx], ux1_recv.at[dx])
        total = total + rx1[dx].astype(F32)
    total = total.astype(BF16).reshape(turns, ys, shard_rows, LANES)
    for yy in range(ys):
        sum_x[yy] = total[:, yy]
    for dy in near_y:
        to = (y + dy) % ys
        send(sum_x.at[to], ry2.at[dy], u_send, uy2_recv.at[dy], me.at(y=to))
    total = term_y[y].astype(F32)
    for dy in near_y:
        wait(ry1.at[dy], uy1_recv.at[dy])
        total = total + ry1[dy].astype(F32)
    sum_y[...] = total.astype(BF16)
    for dx in near_x:
        to = (x + dx) % xs
        send(sum_y.at[to], rx2.at[dx], u_send, ux2_recv.at[dx], me.at(x=to))

    @pl.when(c == 0)
    def _():
        wait(wd, local_sem.at[1])

    @pl.when(c == 1)
    def _():
        wait(wd, pair_recv.at[3])

    def in_rows(xb):
        span = pl.ds(xb * block, block)
        in_grad[:, span] = sum(
            dot(grad[:, col * LANES : (col + 1) * LANES], wd[col, span], 1, 1) for col in range(ys)
        ).astype(BF16)

    for xb in range(xs // 2):
        in_rows(xb)

    total = sum_x[y].astype(F32)
    for dy in near_y:
        wait(ry2.at[dy], uy2_recv.at[dy])
        total = total + ry2[dy].astype(F32)
    s2[:, :, :LANES] = total.astype(BF16)
    total = sum_y[x].astype(F32)
    for dx in near_x:
        wait(rx2.at[dx], ux2_recv.at[dx])
        total = total + rx2[dx].astype(F32)
    s2[:, :, LANES:] = total.astype(BF16)

    def up_grad_sent():
        for _ in near_x:
            wait(term_x.at[0], u_send)
            wait(term_y.at[0], u_send)
            wait(sum_x.at[0], u_send)
            wait(sum_y.at[0], u_send)

    due["up_grad"] = up_grad_sent

    owner = z % ys == y
    for q in range(turns):
        to = q * ys + y

        @pl.when(to != z)
        def _():
            send(s2.at[q], rz.at[z], uz_send, uz_recv, me.at(z=to))

        @pl.when(to == z)
        def _():
            rz[z] = s2[q]

    for xb in range(xs // 2, xs):
        in_rows(xb)

    @pl.when(owner)
    def _():
        wait(rz.at[pl.ds(0, zs - 1)], uz_recv)
        total = rz[0].astype(F32)
        for source in range(1, zs):
            total = total + rz[source].astype(F32)
        shared[c] = (total * scale).astype(BF16)
        for dy in near_y + (0,):
            for dc in range(CORES):
                if dy or dc:
                    send(
                        shared.at[c], shared.at[c], uo_send, uo_recv.at[c],
                        me.at(y=(y + dy) % ys, c=(c + dc) % CORES),
                    )
        for _ in range(ys * CORES - 1):
            wait(shared.at[c], uo_send)
        wait(s2.at[pl.ds(0, turns - 1)], uz_send)
        wait(shared.at[other], uo_recv.at[other])

    @pl.when(jnp.logical_not(owner))
    def _():
        for core in range(CORES):
            wait(shared.at[core], uo_recv.at[core])
        wait(s2, uz_send)

    for core in range(CORES):
        up_grad[:, core * wide : (core + 1) * wide] = shared[core].astype(F32)

    take(*list(due))


def local(
    sizes,
    tokens,
    gate_values,
    expert_ids,
    down_weight,
    up_weight,
    expert_gate,
    expert_up,
    expert_down,
    out_grad,
):
    xs, ys, zs = sizes
    experts = xs * zs
    tok, width = tokens.shape
    top = expert_ids.shape[1]
    turns = zs // ys
    shard_rows, latent = down_weight.shape
    hidden = expert_gate.shape[2]
    cap = max(2, 4 * tok * top // (3 * experts))
    plane = experts // SLAB
    slots = plane * cap
    total_tokens = tok * ys * CORES * experts
    block = shard_rows * zs
    wide = latent // CORES
    vmem = pl.BlockSpec(memory_space=pltpu.VMEM)
    hbm = pl.BlockSpec(memory_space=pl.ANY)
    dma = pltpu.SemaphoreType.DMA

    def held(*shape, kind=BF16):
        return pltpu.VMEM(shape, kind)

    return pl.pallas_call(
        functools.partial(layer_kernel, sizes, cap, 1.0 / math.sqrt(total_tokens)),
        out_shape=(
            jax.ShapeDtypeStruct((tok, width), BF16),
            jax.ShapeDtypeStruct((shard_rows, latent), F32),
        ),
        in_specs=[hbm, hbm, vmem, vmem, vmem, vmem, hbm, hbm, hbm],
        out_specs=(vmem, vmem),
        scratch_shapes=[
            held(ys, width, LANES),
            held(ys, width, LANES),
            held(CORES * tok, width),
            held(CORES * tok, width),
            held(width, CORES * tok),
            held(ys, CORES * tok, LANES),
            held(SLAB, tok, 2 * latent),
            held(SLAB, top, tok, kind=F32),
            held(SLAB, top, tok, kind=jnp.int32),
            held(SLAB + 1, slots, tok),
            held(SLAB + 1, slots, tok),
            held(SLAB + 1, slots, tok),
            held(SLAB, plane, cap, 2 * latent),
            held(plane, SLAB, cap, 2 * latent),
            held(latent, hidden),
            held(latent, hidden),
            held(hidden, latent),
            held(SLAB * slots, hidden, kind=F32),
            held(SLAB * slots, hidden, kind=F32),
            held(SLAB * slots, hidden),
            held(plane, SLAB, cap, latent),
            held(plane, SLAB, cap, latent),
            held(SLAB, plane, cap, latent),
            held(SLAB, plane, cap, latent),
            held(CORES * tok, latent),
            held(xs, block, LANES),
            held(ys, xs, turns, shard_rows, LANES),
            held(xs, block, LANES),
            held(ys, xs, turns, shard_rows, LANES),
            held(ys, turns, shard_rows, LANES),
            held(xs, turns, shard_rows, LANES),
            held(xs, turns, shard_rows, LANES),
            held(ys, turns, shard_rows, LANES),
            held(turns, shard_rows, wide),
            held(zs, shard_rows, wide),
            held(CORES, shard_rows, wide),
            dma((3,)), dma((5,)), dma((5,)), dma(()), dma(()),
            dma(()), dma((xs,)), dma((ys,)), dma((ys,)), dma((xs,)), dma((WINDOW, 2)), dma(()), dma((2 * CHUNKS + LAST,)),
            dma((3,)), dma((3,)), dma(()), dma(()), dma((2, 2)), dma((2, 2)),
            dma(()), dma((xs,)), dma((ys,)), dma((xs,)), dma((ys,)), dma(()), dma(()), dma(()), dma((CORES,)),
        ],
        compiler_params=pltpu.CompilerParams(
            has_side_effects=True, collective_id=0, vmem_limit_bytes=56 * 2**20
        ),
        name="layer",
    )(tokens, out_grad, gate_values.T, expert_ids.T, down_weight, up_weight, expert_gate, expert_up, expert_down)


def solution(mesh):
    dp, ex = mesh.shape["dp"], mesh.shape["expert"]
    ys = dp // CORES
    sizes = (ys, ys, ex // ys)
    return jax.shard_map(
        functools.partial(local, sizes),
        mesh=mesh,
        in_specs=(
            P(("dp", "expert"), None),
            P(("dp", "expert"), None),
            P(("dp", "expert"), None),
            P("expert", None),
            P("expert", None),
            P("expert", None, None),
            P("expert", None, None),
            P("expert", None, None),
            P(("dp", "expert"), None),
        ),
        out_specs=(P(("dp", "expert"), None), P("expert", None)),
        check_vma=False,
    )
```

```python
import functools
import math

import jax
import jax.numpy as jnp
from jax import lax
from jax.experimental import pallas as pl
from jax.experimental.pallas import tpu as pltpu
from jax.sharding import PartitionSpec as P

CORES = 2
SLAB = 2
LANES = 128
CHUNKS = 8
LAST = 16
LAG = 2
IN_RING = 3
IN_PLANE = 1
IN_WAIT = 1
IN_PRODUCT = 2
BATCH = 16
WINDOW = 2
AHEAD = 3
F32 = jnp.float32
BF16 = jnp.bfloat16


class Place:
    def __init__(self, sizes):
        self.xs, self.ys, self.zs = sizes
        dp, ex = lax.axis_index("dp"), lax.axis_index("expert")
        self.y, self.c = dp // CORES, dp % CORES
        self.x, self.z = ex // self.zs, ex % self.zs
        self.half = self.z % SLAB
        self.index = (self.x * self.ys + self.y) * CORES + self.c
        self.plane = self.xs * self.ys * CORES

    def at(self, x=None, y=None, z=None, c=None):
        x = self.x if x is None else x
        y = self.y if y is None else y
        z = self.z if z is None else z
        c = self.c if c is None else c
        return (y * CORES + c, x * self.zs + z)

    def in_plane(self, index, z=None):
        c, y, x = index % CORES, index // CORES % self.ys, index // (CORES * self.ys)
        return self.at(x=x, y=y, z=z, c=c)


def send(src, dst, send_sem, recv_sem, device):
    pltpu.make_async_remote_copy(
        src_ref=src,
        dst_ref=dst,
        send_sem=send_sem,
        recv_sem=recv_sem,
        device_id=device,
        device_id_type=pl.DeviceIdType.MESH,
    ).start()


def wait(ref, sem):
    pltpu.make_async_copy(ref, ref, sem).wait()


def rows(start, size):
    return pl.ds(pl.multiple_of(start, size), size)


def dot(left, right, left_axis=1, right_axis=0):
    return lax.dot_general(
        left, right, (((left_axis,), (right_axis,)), ((), ())), preferred_element_type=F32
    )


class Weights:
    def __init__(self, me, pairs, own_sem, send_sem, recv_sem):
        self.me, self.pairs = me, pairs
        self.own_sem, self.send_sem, self.recv_sem = own_sem, send_sem, recv_sem
        zs = me.zs
        base = me.z + zs - me.y - zs // (CORES * SLAB) * me.c
        which = base % zs // (zs // SLAB)
        away = (base + zs - (zs // SLAB) * me.half) % zs
        self.owns = base % (zs // SLAB) == 0
        self.same = jnp.logical_and(self.owns, which == me.half)
        self.first = jnp.where(which == me.half, 2, 1)
        up = jnp.logical_and(away > 0, away + 2 <= zs // 2 - me.c)
        self.passes = jnp.logical_or(up, away > zs // 2 + 2 - me.c)
        self.hop = (jnp.where(up, away, zs - away) + 1) // 2
        self.hops = zs // 4 - 1
        self.next = me.at(z=(me.z + jnp.where(up, 2, zs - 2)) % zs)
        self.counts = (CHUNKS, CHUNKS, LAST)
        self.total = sum(self.counts)
        self.begun = self.arrived = self.point = 0
        self.passed = [0] * self.hops
        self.begin(WINDOW)

    def piece(self, i):
        matrix = 0
        while i >= self.counts[matrix]:
            i -= self.counts[matrix]
            matrix += 1
        src, dst = self.pairs[matrix]
        size = dst.shape[0] // self.counts[matrix]
        part = pl.ds(i * size, size)
        return src.at[0, part], dst.at[part]

    def begin(self, upto):
        me = self.me
        upto = min(upto, self.total)
        todo = range(self.begun, upto)
        self.begun = max(self.begun, upto)
        if not todo:
            return

        @pl.when(self.same)
        def _():
            for i in todo:
                src, dst = self.piece(i)
                pltpu.make_async_copy(src, dst, self.recv_sem.at[i]).start()

        @pl.when(self.owns)
        def _():
            for i in todo:
                src, dst = self.piece(i)
                for way, ahead in enumerate((self.first, me.zs - self.first)):
                    sent = self.own_sem.at[i % WINDOW, way]
                    if i >= WINDOW:
                        wait(self.piece(i - WINDOW)[1], sent)
                    send(src, dst, sent, self.recv_sem.at[i], me.at(z=(me.z + ahead) % me.zs))

    def hand_on(self, number, upto):
        todo = range(self.passed[number], min(upto, self.total))
        self.passed[number] = max(self.passed[number], min(upto, self.total))
        if not todo:
            return

        @pl.when(jnp.logical_and(self.passes, self.hop == number + 1))
        def _():
            for i in todo:
                dst = self.piece(i)[1]
                wait(dst, self.recv_sem.at[i])
                send(dst, dst, self.send_sem, self.recv_sem.at[i], self.next)

    def step(self, count=1):
        self.point += count
        self.begin(self.point + AHEAD)
        for number in range(self.hops):
            self.hand_on(number, self.point - LAG * number)

    def arrive(self, matrices=None):
        upto = sum(self.counts[:matrices])
        self.begin(upto + AHEAD)
        for number in range(self.hops):
            self.hand_on(number, upto)
        self.point = max(self.point, upto)
        todo = range(self.arrived, upto)
        self.arrived = upto

        @pl.when(jnp.logical_not(self.passes))
        def _():
            for i in todo:
                wait(self.piece(i)[1], self.recv_sem.at[i])

    def finish(self):
        @pl.when(self.owns)
        def _():
            for i in range(self.total - WINDOW, self.total):
                for way in range(2):
                    wait(self.piece(i)[1], self.own_sem.at[i % WINDOW, way])

        @pl.when(self.passes)
        def _():
            for _, dst in self.pairs:
                wait(dst, self.send_sem)


def layer_kernel(
    sizes, cap, scale,
    tokens, out_grad, gates, ids, down, up, w_gate, w_up, w_down,
    in_grad, up_grad,
    w4, wd, both, og, ogt, res, lc, gate2, ids2, pick, weight, outbox, inbox, wg, wu, wn,
    gate_pre, up_pre, hid, result, back, ret, ret2, cb,
    term_x, term_y, rx1, ry1, sum_x, sum_y, rx2, ry2, s2, rz, shared,
    local_sem, pair_send, pair_recv, z_send, z_recv, g_send, ax_recv, by_recv, ay_recv, bx_recv, w_own, w_send, w_recv,
    n_send, n_recv, s_send, s_recv, r_send, r_recv,
    u_send, ux1_recv, uy1_recv, ux2_recv, uy2_recv, uz_send, uz_recv, uo_send, uo_recv,
):
    me = Place(sizes)
    xs, ys, zs = sizes
    x, y, z, c, half = me.x, me.y, me.z, me.c, me.half
    other = 1 - c
    shard_rows, latent = down.shape
    tok, width = tokens.shape
    block = shard_rows * zs
    sub = block // 2
    peer = me.at(c=other)
    partner_z = z + 1 - 2 * half
    partner = me.at(z=partner_z)
    plane = me.plane
    top = ids.shape[0]
    mine = rows(c * tok, tok)
    near_x = (1, xs - 1) + tuple(range(2, xs - 1))
    near_y = (1, ys - 1) + tuple(range(2, ys - 1))
    due = {}

    def take(*names):
        for name in names:
            due.pop(name)()

    def owe(name, ref, sem, when=None):
        if when is None:
            due[name] = lambda: wait(ref, sem)
        else:
            due[name] = lambda: pl.when(when)(lambda: wait(ref, sem))

    barrier = pltpu.get_barrier_semaphore()

    def greet(device):
        pl.semaphore_signal(barrier, inc=1, device_id=device, device_id_type=pl.DeviceIdType.MESH)

    def greet_plane(d, _):
        greet(me.in_plane((me.index + d) % plane))
        return 0

    def greet_next(d, _):
        greet(me.in_plane(d, partner_z))
        return 0

    def greet_ring(d, _):
        to = (z + d) % zs

        @pl.when(to != partner_z)
        def _():
            greet(me.at(z=to))

        return 0

    lax.fori_loop(1, zs, greet_ring, 0)
    lax.fori_loop(1, plane, greet_plane, 0)
    lax.fori_loop(0, plane, greet_next, 0)

    @pl.when(c == 0)
    def _():
        pltpu.make_async_copy(tokens, both.at[mine], local_sem.at[0]).start()
        w4[y, rows((x * zs + z) * shard_rows, shard_rows)] = down[:, pl.ds(pl.multiple_of(y * LANES, LANES), LANES)]

    @pl.when(c == 1)
    def _():
        pltpu.make_async_copy(out_grad, both.at[mine], local_sem.at[0]).start()
        w4[y, rows((x * zs + z) * shard_rows, shard_rows)] = up[:, pl.ds(pl.multiple_of(y * LANES, LANES), LANES)]

    pltpu.make_async_copy(out_grad, og.at[mine], local_sem.at[2]).start()
    gate2[half] = gates[...]
    ids2[half] = ids[...]

    slots = plane * cap
    row = lax.broadcasted_iota(jnp.int32, (slots, 1), 0)
    seat, index = (row % cap).astype(F32), row // cap
    at_even = (
        index // (CORES * ys) * zs + index // CORES % ys + zs // (CORES * SLAB) * (index % CORES)
    )
    before = (
        lax.broadcasted_iota(jnp.int32, (tok, tok), 0) < lax.broadcasted_iota(jnp.int32, (tok, tok), 1)
    ).astype(BF16)

    def seats(table, q, which):
        expert = at_even + (zs // SLAB) * which
        named = jnp.zeros((slots, tok), F32)
        gate = jnp.zeros((slots, tok), F32)
        for k in range(top):
            hit = ids2[q, k : k + 1, :] == expert
            named = jnp.where(hit, 1.0, named)
            gate = jnp.where(hit, gate2[q, k : k + 1, :], gate)
        chosen = jnp.where(dot(named.astype(BF16), before) == seat, named, 0.0)
        pick[table] = chosen.astype(BF16)
        weight[table] = (gate * chosen).astype(BF16)

    seats(0, half, half)

    pl.semaphore_wait(barrier, 2 * plane - 1 + zs - 2)

    piece = w4.at[y, rows((x * zs + z) * shard_rows, shard_rows)]
    for dz in range(1, zs):
        send(piece, piece, z_send, z_recv, me.at(z=(z + dz) % zs))
    others = w4.at[0, pl.ds(0, block - shard_rows)]
    owe("z_send", others, z_send)
    send(gates, gate2.at[half], n_send.at[0], n_recv.at[0], partner)
    send(ids, ids2.at[half], n_send.at[1], n_recv.at[1], partner)
    owe("gates", gates, n_send.at[0])
    owe("ids", ids, n_send.at[1])

    @pl.when(c == 0)
    def _():
        send(out_grad, both.at[mine], pair_send.at[0], pair_recv.at[0], peer)

    @pl.when(c == 1)
    def _():
        send(tokens, both.at[mine], pair_send.at[0], pair_recv.at[0], peer)

    owe("both", both.at[mine], pair_send.at[0])
    weights = Weights(me, ((w_gate, wg), (w_up, wu), (w_down, wn)), w_own, w_send, w_recv)
    send(out_grad, og.at[mine], pair_send.at[2], pair_recv.at[2], peer)
    owe("og", og.at[mine], pair_send.at[2])
    weights.step(IN_RING)
    wait(others, z_recv)

    def first_rows(xx):
        return rows(xx * block, sub)

    def second_rows(xx):
        return rows(xx * block + sub, sub)

    def away(at, size, d):
        return (at + size - d) % size

    for dx, dy in zip(near_x, near_y):
        a, b = w4.at[y, first_rows(x)], w4.at[y, second_rows(x)]
        send(a, a, g_send, ax_recv.at[dx], me.at(x=(x + dx) % xs))
        send(b, b, g_send, by_recv.at[dy], me.at(y=(y + dy) % ys))
    for step in range(xs):
        dx, dy = ((0,) + near_x)[step], ((0,) + near_y)[step]
        a = w4.at[y, first_rows(away(x, xs, dx))]
        b = w4.at[away(y, ys, dy), second_rows(x)]
        if step:
            wait(a, ax_recv.at[dx])
            wait(b, by_recv.at[dy])
        for to_x, to_y in zip(near_x, near_y):
            send(a, a, g_send, ay_recv.at[to_y], me.at(y=(y + to_y) % ys))
            send(b, b, g_send, bx_recv.at[to_x], me.at(x=(x + to_x) % xs))
        weights.step(IN_PLANE)

    def all_gathered():
        for _ in range(2 * (xs - 1)):
            wait(w4.at[0, pl.ds(0, sub)], g_send)
            wait(w4.at[0, pl.ds(0, xs * sub)], g_send)

    due["gather"] = all_gathered

    wait(gates, n_recv.at[0])
    wait(ids, n_recv.at[1])
    seats(1, 1 - half, half)
    seats(2, half, 1 - half)

    for dx, dy in zip(near_x, near_y):
        wait(w4.at[0, pl.ds(0, xs * sub)], ay_recv.at[dy])
        wait(w4.at[0, pl.ds(0, ys * sub)], bx_recv.at[dx])
        weights.step(IN_WAIT)

    wait(both.at[mine], local_sem.at[0])
    wait(both.at[mine], pair_recv.at[0])

    def lanes(col):
        return pl.ds(pl.multiple_of(c * latent + col * LANES, LANES), LANES)

    for col in range(ys):
        res[col] = dot(both[...], w4[col]).astype(BF16)
        theirs, place = res.at[col, rows(other * tok, tok)], lc.at[half, :, lanes(col)]
        send(res.at[col, mine], place, n_send.at[2], n_recv.at[2], partner)
        send(theirs, place, n_send.at[2], n_recv.at[2], me.at(z=partner_z, c=other))
        send(theirs, place, pair_send.at[1], pair_recv.at[1], peer)
    for col in range(ys):
        lc[half, :, lanes(col)] = res[col, mine, :]
    quarter = lc.at[half, :, pl.ds(0, latent)]
    owe("quarter", quarter, pair_send.at[1])

    @pl.when(c == 0)
    def _():
        send(w4, wd, pair_send.at[3], pair_recv.at[3], peer)
        pltpu.make_async_copy(w4, wd, local_sem.at[1]).start()

    owe("wd", wd, pair_send.at[3], c == 0)
    weights.step(IN_PRODUCT)
    wait(quarter, pair_recv.at[1])
    owe("lc", lc.at[0], n_send.at[2])

    def dispatch(table, q):
        tile = 8

        def fill(t, _):
            span = rows(t * tile * cap, tile * cap)
            picked = dot(pick[table, span], lc[q, :, :latent])
            cot = dot(weight[table, span], lc[q, :, latent:])
            outbox[q, pl.ds(t * tile, tile), :, :latent] = picked.astype(BF16).reshape(tile, cap, latent)
            outbox[q, pl.ds(t * tile, tile), :, latent:] = cot.astype(BF16).reshape(tile, cap, latent)
            return 0

        lax.fori_loop(0, plane // tile, fill, 0)

        def post(d, _):
            to = (me.index + d) % plane
            send(outbox.at[q, to], inbox.at[me.index, q], s_send, s_recv, me.in_plane(to))
            return 0

        for start in range(1, plane, BATCH):
            lax.fori_loop(start, min(start + BATCH, plane), post, 0)
            weights.step()
        inbox[me.index, q] = outbox[q, me.index]

    dispatch(0, half)
    wait(lc.at[0], n_recv.at[2])
    dispatch(1, 1 - half)
    owe("inbox", inbox.at[pl.ds(0, plane - 1)], s_send)
    wait(og.at[mine], local_sem.at[2])
    wait(og.at[mine], pair_recv.at[2])
    for xb in range(xs):
        ogt[pl.ds(xb * block, block), :] = og[:, pl.ds(xb * block, block)].T
        weights.step()
    weights.arrive(2)
    wait(inbox.at[pl.ds(0, plane - 1)], s_recv)

    group = 8
    size = group * SLAB * cap

    def tile_of(t):
        return (t + me.index // group) % (plane // group)

    def post_back(box, ret_box, which, g):
        def post(d, _):
            to = g * group + d

            send(
                box.at[to, 1 - half], ret_box.at[half, me.index],
                r_send.at[which, 1], r_recv.at[which, 1], me.in_plane(to, partner_z),
            )

            @pl.when(to != me.index)
            def _():
                send(
                    box.at[to, half], ret_box.at[half, me.index],
                    r_send.at[which, 0], r_recv.at[which, 0], me.in_plane(to),
                )

            @pl.when(to == me.index)
            def _():
                ret_box[half, to] = box[to, half]

            return 0

        lax.fori_loop(0, group, post, 0)

    def before_hidden(t):
        g = tile_of(t)
        box, span = pl.ds(g * group, group), rows(g * size, size)
        value = inbox[box, :, :, :latent].reshape(size, latent)
        pre = dot(value, wg[...])
        pre_up = dot(value, wu[...])
        gate_pre[span, :] = pre
        up_pre[span, :] = pre_up
        hid[span, :] = (pre * jax.nn.sigmoid(pre) * pre_up).astype(BF16)

    for t in range(plane // group):
        before_hidden(t)
        weights.step(2)
    weights.arrive()
    due["weights"] = weights.finish

    def forward(t, _):
        g = tile_of(t)
        box, span = pl.ds(g * group, group), rows(g * size, size)
        result[box] = dot(hid[span, :], wn[...]).astype(BF16).reshape(group, SLAB, cap, latent)
        post_back(result, ret, 0, g)
        return 0

    lax.fori_loop(0, plane // group, forward, 0)

    def backward(t, _):
        g = tile_of(t)
        box, span = pl.ds(g * group, group), rows(g * size, size)
        value = inbox[box, :, :, latent:].reshape(size, latent)
        hidden_cot = dot(value, wn[...], 1, 1)
        pre, pre_up = gate_pre[span, :], up_pre[span, :]
        sig = jax.nn.sigmoid(pre)
        gate_cot = (hidden_cot * pre_up * sig * (1.0 + pre * (1.0 - sig))).astype(BF16)
        up_cot = (hidden_cot * pre * sig).astype(BF16)
        total = dot(gate_cot, wg[...], 1, 1) + dot(up_cot, wu[...], 1, 1)
        back[box] = total.astype(BF16).reshape(group, SLAB, cap, latent)
        post_back(back, ret2, 1, g)
        return 0

    lax.fori_loop(0, plane // group, backward, 0)
    for which, box in enumerate((ret, ret2)):
        owe(f"back{which}", box.at[0, pl.ds(0, plane - 1)], r_send.at[which, 0])
        owe(f"next{which}", box.at[0], r_send.at[which, 1])

    def sum_back(which, box, table_of):
        wait(box.at[0, pl.ds(0, plane - 1)], r_recv.at[which, 0])
        wait(box.at[0], r_recv.at[which, 1])
        total = jnp.zeros((tok, latent), F32)
        for table, plane_half in ((0, half), (2, 1 - half)):
            value = box[plane_half].reshape(slots, latent)
            total = total + dot(table_of[table], value, 0, 0)
        return total.astype(BF16)

    cb[mine, :] = sum_back(0, ret, weight)
    send(cb.at[mine], cb.at[mine], pair_send.at[4], pair_recv.at[4], peer)
    owe("cb", cb.at[mine], pair_send.at[4])
    wait(cb.at[mine], pair_recv.at[4])

    wide = latent // CORES
    cols = pl.ds(pl.multiple_of(c * wide, LANES), wide)
    columns = cb[:, cols]
    turns = zs // ys
    for dx in near_x + (0,):
        to = (x + dx) % xs
        value = dot(ogt[rows(to * block, block), :], columns).astype(BF16)
        term_x[dx] = value[:, :LANES]
        if dx:
            send(term_x.at[dx], rx1.at[dx], u_send, ux1_recv.at[dx], me.at(x=to))
        second = value[:, LANES:].reshape(turns, ys, shard_rows, LANES)
        for yy in range(ys):
            term_y[yy, to] = second[:, yy]
    for dy in near_y:
        to = (y + dy) % ys
        send(term_y.at[to], ry1.at[dy], u_send, uy1_recv.at[dy], me.at(y=to))

    grad = sum_back(1, ret2, pick)
    total = term_x[0].astype(F32)
    for dx in near_x:
        wait(rx1.at[dx], ux1_recv.at[dx])
        total = total + rx1[dx].astype(F32)
    total = total.astype(BF16).reshape(turns, ys, shard_rows, LANES)
    for yy in range(ys):
        sum_x[yy] = total[:, yy]
    for dy in near_y:
        to = (y + dy) % ys
        send(sum_x.at[to], ry2.at[dy], u_send, uy2_recv.at[dy], me.at(y=to))
    total = term_y[y].astype(F32)
    for dy in near_y:
        wait(ry1.at[dy], uy1_recv.at[dy])
        total = total + ry1[dy].astype(F32)
    sum_y[...] = total.astype(BF16)
    for dx in near_x:
        to = (x + dx) % xs
        send(sum_y.at[to], rx2.at[dx], u_send, ux2_recv.at[dx], me.at(x=to))

    @pl.when(c == 0)
    def _():
        wait(wd, local_sem.at[1])

    @pl.when(c == 1)
    def _():
        wait(wd, pair_recv.at[3])

    def in_rows(xb):
        span = pl.ds(xb * block, block)
        in_grad[:, span] = sum(
            dot(grad[:, col * LANES : (col + 1) * LANES], wd[col, span], 1, 1) for col in range(ys)
        ).astype(BF16)

    for xb in range(xs // 2):
        in_rows(xb)

    total = sum_x[y].astype(F32)
    for dy in near_y:
        wait(ry2.at[dy], uy2_recv.at[dy])
        total = total + ry2[dy].astype(F32)
    s2[:, :, :LANES] = total.astype(BF16)
    total = sum_y[x].astype(F32)
    for dx in near_x:
        wait(rx2.at[dx], ux2_recv.at[dx])
        total = total + rx2[dx].astype(F32)
    s2[:, :, LANES:] = total.astype(BF16)

    def up_grad_sent():
        for _ in near_x:
            wait(term_x.at[0], u_send)
            wait(term_y.at[0], u_send)
            wait(sum_x.at[0], u_send)
            wait(sum_y.at[0], u_send)

    due["up_grad"] = up_grad_sent

    owner = z % ys == y
    for q in range(turns):
        to = q * ys + y

        @pl.when(to != z)
        def _():
            send(s2.at[q], rz.at[z], uz_send, uz_recv, me.at(z=to))

        @pl.when(to == z)
        def _():
            rz[z] = s2[q]

    for xb in range(xs // 2, xs):
        in_rows(xb)

    @pl.when(owner)
    def _():
        wait(rz.at[pl.ds(0, zs - 1)], uz_recv)
        total = rz[0].astype(F32)
        for source in range(1, zs):
            total = total + rz[source].astype(F32)
        shared[c] = (total * scale).astype(BF16)
        for dy in near_y + (0,):
            for dc in range(CORES):
                if dy or dc:
                    send(
                        shared.at[c], shared.at[c], uo_send, uo_recv.at[c],
                        me.at(y=(y + dy) % ys, c=(c + dc) % CORES),
                    )
        for _ in range(ys * CORES - 1):
            wait(shared.at[c], uo_send)
        wait(s2.at[pl.ds(0, turns - 1)], uz_send)
        wait(shared.at[other], uo_recv.at[other])

    @pl.when(jnp.logical_not(owner))
    def _():
        for core in range(CORES):
            wait(shared.at[core], uo_recv.at[core])
        wait(s2, uz_send)

    for core in range(CORES):
        up_grad[:, core * wide : (core + 1) * wide] = shared[core].astype(F32)

    take(*list(due))


def local(
    sizes,
    tokens,
    gate_values,
    expert_ids,
    down_weight,
    up_weight,
    expert_gate,
    expert_up,
    expert_down,
    out_grad,
):
    xs, ys, zs = sizes
    experts = xs * zs
    tok, width = tokens.shape
    top = expert_ids.shape[1]
    turns = zs // ys
    shard_rows, latent = down_weight.shape
    hidden = expert_gate.shape[2]
    cap = max(2, 4 * tok * top // (3 * experts))
    plane = experts // SLAB
    slots = plane * cap
    total_tokens = tok * ys * CORES * experts
    block = shard_rows * zs
    wide = latent // CORES
    vmem = pl.BlockSpec(memory_space=pltpu.VMEM)
    hbm = pl.BlockSpec(memory_space=pl.ANY)
    dma = pltpu.SemaphoreType.DMA

    def held(*shape, kind=BF16):
        return pltpu.VMEM(shape, kind)

    return pl.pallas_call(
        functools.partial(layer_kernel, sizes, cap, 1.0 / math.sqrt(total_tokens)),
        out_shape=(
            jax.ShapeDtypeStruct((tok, width), BF16),
            jax.ShapeDtypeStruct((shard_rows, latent), F32),
        ),
        in_specs=[hbm, hbm, vmem, vmem, vmem, vmem, hbm, hbm, hbm],
        out_specs=(vmem, vmem),
        scratch_shapes=[
            held(ys, width, LANES),
            held(ys, width, LANES),
            held(CORES * tok, width),
            held(CORES * tok, width),
            held(width, CORES * tok),
            held(ys, CORES * tok, LANES),
            held(SLAB, tok, 2 * latent),
            held(SLAB, top, tok, kind=F32),
            held(SLAB, top, tok, kind=jnp.int32),
            held(SLAB + 1, slots, tok),
            held(SLAB + 1, slots, tok),
            held(SLAB, plane, cap, 2 * latent),
            held(plane, SLAB, cap, 2 * latent),
            held(latent, hidden),
            held(latent, hidden),
            held(hidden, latent),
            held(SLAB * slots, hidden, kind=F32),
            held(SLAB * slots, hidden, kind=F32),
            held(SLAB * slots, hidden),
            held(plane, SLAB, cap, latent),
            held(plane, SLAB, cap, latent),
            held(SLAB, plane, cap, latent),
            held(SLAB, plane, cap, latent),
            held(CORES * tok, latent),
            held(xs, block, LANES),
            held(ys, xs, turns, shard_rows, LANES),
            held(xs, block, LANES),
            held(ys, xs, turns, shard_rows, LANES),
            held(ys, turns, shard_rows, LANES),
            held(xs, turns, shard_rows, LANES),
            held(xs, turns, shard_rows, LANES),
            held(ys, turns, shard_rows, LANES),
            held(turns, shard_rows, wide),
            held(zs, shard_rows, wide),
            held(CORES, shard_rows, wide),
            dma((3,)), dma((5,)), dma((5,)), dma(()), dma(()),
            dma(()), dma((xs,)), dma((ys,)), dma((ys,)), dma((xs,)), dma((WINDOW, 2)), dma(()), dma((2 * CHUNKS + LAST,)),
            dma((3,)), dma((3,)), dma(()), dma(()), dma((2, 2)), dma((2, 2)),
            dma(()), dma((xs,)), dma((ys,)), dma((xs,)), dma((ys,)), dma(()), dma(()), dma(()), dma((CORES,)),
        ],
        compiler_params=pltpu.CompilerParams(
            has_side_effects=True, collective_id=0, vmem_limit_bytes=56 * 2**20
        ),
        name="layer",
    )(tokens, out_grad, gate_values.T, expert_ids.T, down_weight, up_weight, expert_gate, expert_up, expert_down)


def solution(mesh):
    dp, ex = mesh.shape["dp"], mesh.shape["expert"]
    ys = dp // CORES
    sizes = (ys, ys, ex // ys)
    return jax.shard_map(
        functools.partial(local, sizes),
        mesh=mesh,
        in_specs=(
            P(("dp", "expert"), None),
            P(("dp", "expert"), None),
            P(("dp", "expert"), None),
            P("expert", None),
            P("expert", None),
            P("expert", None, None),
            P("expert", None, None),
            P("expert", None, None),
            P(("dp", "expert"), None),
        ),
        out_specs=(P(("dp", "expert"), None), P("expert", None)),
        check_vma=False,
    )
```
